256 devices in a mesh: ctx: 32 (over y_lo, z, core), tp: 8 (over y_hi, x).
Axes of the slice: x: 4, y: 4 (y_hi: 2, y_lo: 2; y = y_hi * 2 + y_lo), z: 8, core: 2. Of those that a mesh axis runs over, the one named last changes fastest.
Arguments:
- queries: bfloat16 [8192, 4096], P('ctx', 'tp'), may hold values from -25 to 25
- keys_values: bfloat16 [8192, 2048], P('ctx', 'tp'), may hold values from -5 to 5
- upstream: bfloat16 [8192, 4096], P('ctx', 'tp'), may hold values from -6 to 6
- out_proj: bfloat16 [4096, 4096], P('ctx', 'tp'), may hold values from -0.09375 to 0.09375
- keep_index: int32 [6144], P('ctx'), may hold values from -1 to 255, as said below
Outputs:
- query_grad: bfloat16 [8192, 4096], P('ctx', 'tp')
- kv_grad: bfloat16 [8192, 2048], P('ctx', 'tp')
- out_proj_grad: bfloat16 [4096, 4096], P('ctx', 'tp')
The draws below stay inside these ranges and needn't reach their ends.
Inputs may be any that keep to these rules, and one draw needn't show every extreme that they name: `keep_index`: each shard's 192 entries list distinct local positions of its kept tokens in ascending order, then -1 in the unused slots; a shard keeps 192 // 3 to 192 tokens, and some shard keeps exactly 192.
All inputs are finite; a program needn't handle non-finite values.
Results may differ from the reference program's by a relative error of at most 0.04.
Values may be sent and summed in bfloat16 or wider, within the bound.
A program may use at most 64 MiB of HBM per device.

```python
import math
import jax
import jax.numpy as jnp
from jax import lax

D = 4096
QUERY_HEADS = 32
KEY_VALUE_HEADS = 8
HEAD_SIZE = 128
TOK_DEV = 256
CAP = 192
SEQUENCE_TOKENS = 8192


def kept_slots(key):
    key = jax.random.fold_in(key, 11)
    count_key, pick_key, order_key = jax.random.split(key, 3)
    shard_count = SEQUENCE_TOKENS // TOK_DEV
    counts = jax.random.randint(count_key, (shard_count,), CAP // 3, CAP + 1)
    fullest = jax.random.randint(pick_key, (), 0, shard_count)
    counts = jnp.where(jnp.arange(shard_count) == fullest, CAP, counts)
    places = jnp.arange(TOK_DEV, dtype=jnp.int32)[None, :]
    ranking = jax.random.randint(order_key, (shard_count, TOK_DEV), 0, 1 << 20) * TOK_DEV + places
    ranks = jnp.argsort(jnp.argsort(ranking, axis=1), axis=1)
    chosen = ranks < counts[:, None]
    marked = jnp.where(chosen, places, TOK_DEV + places)
    ordered = jnp.sort(marked, axis=1)[:, :CAP]
    return jnp.where(ordered < TOK_DEV, ordered, -1).astype(jnp.int32)


def draw_keep_index(key, part):
    return kept_slots(key).reshape(-1)


def draw_queries(key, part):
    key = jax.random.fold_in(key, 13)
    value_rows = jnp.clip(jax.random.normal(key, (SEQUENCE_TOKENS, QUERY_HEADS * HEAD_SIZE), jnp.float32), -5.0, 5.0)
    return value_rows.astype(jnp.bfloat16)


def draw_keys_values(key, part):
    key = jax.random.fold_in(key, 14)
    value_rows = jnp.clip(jax.random.normal(key, (SEQUENCE_TOKENS, KEY_VALUE_HEADS * 2 * HEAD_SIZE), jnp.float32), -5.0, 5.0)
    return value_rows.astype(jnp.bfloat16)


def with_spikes(values, own_key, source, target, parts, factor):
    def block_of(position):
        return (jnp.arange(values.shape[position]) // (values.shape[position] // parts)).reshape((-1,) + (1,) * (values.ndim - 1 - position))

    one_side = jax.random.permutation(own_key, parts)[block_of(target)]
    other_side = (block_of(target) + parts // 2) % parts
    return jnp.where((block_of(source) == one_side) | (block_of(source) == other_side), factor * values, values)


def level_of(rng, dims, cuts, least, largest):
    def one(dim, blocks):
        heights = jax.random.uniform(jax.random.fold_in(jax.random.fold_in(rng, 6), dim), (blocks,), jnp.float32, least / len(cuts), largest / len(cuts))
        return jnp.repeat(jnp.exp(heights), dims[dim] // blocks).reshape((-1,) + (1,) * (len(dims) - dim - 1))

    factor_of = one(*cuts[0])
    for cut in cuts[1:]:
        factor_of = factor_of * one(*cut)
    return factor_of


def noise(own_key, shape, width, limit, pieces=(), held_as=jnp.bfloat16):
    values = jax.random.normal(own_key, shape, jnp.float32) * width
    if len(pieces) > 0:
        values = level_of(own_key, shape, pieces, -0.22, 0.18) * values
    return jnp.clip(values, min=-limit, max=limit).astype(held_as)


def noise_with(own_key, extent, spread, most, cuts, heavy, held_as=jnp.bfloat16):
    values = spread * jax.random.normal(own_key, extent, jnp.float32)
    if cuts:
        values = values * level_of(own_key, extent, cuts, -0.22, 0.18)
    return jnp.clip(with_spikes(values, jax.random.fold_in(own_key, 3), *heavy), -most, most).astype(held_as)


def setup_inputs(seed: int = 0) -> dict:
    keys = jax.random.split(jax.random.key(seed), 6)
    return {
        "queries": draw_queries(jax.random.fold_in(keys[5], 71), 0),
        "keys_values": draw_keys_values(jax.random.fold_in(keys[5], 71), 0),
        "upstream": noise_with(keys[2], (SEQUENCE_TOKENS, D), 1.0, 6.0, ((0, 32), (1, 8)), (0, 1, 32, 2.75)),
        "out_proj": noise(keys[3], (D, QUERY_HEADS * HEAD_SIZE), D ** -0.5, 0.09375, ((0, 32), (1, 8))),
        "keep_index": draw_keep_index(jax.random.fold_in(keys[5], 71), 0),
    }


def reference(queries, keys_values, upstream, out_proj, keep_index):
    shard_count = SEQUENCE_TOKENS // TOK_DEV
    query_group_width = QUERY_HEADS // KEY_VALUE_HEADS
    score_scale = 1.0 / math.sqrt(HEAD_SIZE)
    slot_table = keep_index.reshape(shard_count, CAP)
    filled = (slot_table >= 0).reshape(-1)
    token_row_set = (slot_table + (jnp.arange(shard_count, dtype=jnp.int32) * TOK_DEV)[:, None]).reshape(-1)
    token_row_set = jnp.where(filled, token_row_set, 0).astype(jnp.int32)
    query_pos = jnp.where(filled, token_row_set, -1)
    key_pos = jnp.where(filled, token_row_set, 1 << 30)
    filled_column = filled[:, None]
    query_kept = jnp.where(filled_column, queries[token_row_set], 0).astype(jnp.bfloat16)
    kv_kept = jnp.where(filled_column, keys_values[token_row_set], 0).astype(jnp.bfloat16)
    upstream_kept = jnp.where(filled_column, upstream[token_row_set], 0).astype(jnp.bfloat16)
    grad_heads = jnp.dot(upstream_kept, out_proj, preferred_element_type=jnp.float32).astype(jnp.bfloat16)
    allowed = key_pos[None, :] <= query_pos[:, None]

    def head_pass(head_index):
        pair_index = head_index // query_group_width
        query_h = lax.dynamic_slice_in_dim(query_kept, head_index * HEAD_SIZE, HEAD_SIZE, 1)
        grad_h = lax.dynamic_slice_in_dim(grad_heads, head_index * HEAD_SIZE, HEAD_SIZE, 1)
        key_h = lax.dynamic_slice_in_dim(kv_kept, pair_index * 2 * HEAD_SIZE, HEAD_SIZE, 1)
        value_h = lax.dynamic_slice_in_dim(kv_kept, pair_index * 2 * HEAD_SIZE + HEAD_SIZE, HEAD_SIZE, 1)
        scores = jnp.dot(query_h, key_h.T, preferred_element_type=jnp.float32) * score_scale
        scores = jnp.where(allowed, scores, jnp.float32(-1e+30))
        row_max = lax.optimization_barrier(jnp.max(scores, axis=1))
        log_total = row_max + jnp.log(lax.optimization_barrier(jnp.sum(jnp.exp(scores - row_max[:, None]), axis=1)))
        probs_full = jnp.exp(scores - log_total[:, None])
        probability_half = probs_full.astype(jnp.bfloat16)
        attn_h = jnp.dot(probs_full, value_h.astype(jnp.float32), precision=lax.Precision.HIGHEST, preferred_element_type=jnp.float32).astype(jnp.bfloat16)
        delta = lax.optimization_barrier(jnp.sum(grad_h.astype(jnp.float32) * attn_h.astype(jnp.float32), axis=1))
        pushes = jnp.dot(grad_h, value_h.T, preferred_element_type=jnp.float32)
        alibi_slopes = (probs_full * (pushes - delta[:, None]) * score_scale).astype(jnp.bfloat16)
        query_part = jnp.dot(alibi_slopes, key_h, preferred_element_type=jnp.float32)
        key_portion = jnp.dot(alibi_slopes.T, query_h, preferred_element_type=jnp.float32)
        value_portion = jnp.dot(probability_half.T, grad_h, preferred_element_type=jnp.float32)
        return (attn_h, query_part, key_portion, value_portion)
    attn, query_part, key_portion, value_portion = lax.map(head_pass, jnp.arange(QUERY_HEADS, dtype=jnp.int32))
    position_total = shard_count * CAP
    attn_flat = attn.transpose(1, 0, 2).reshape(position_total, QUERY_HEADS * HEAD_SIZE)
    query_flat = query_part.transpose(1, 0, 2).reshape(position_total, QUERY_HEADS * HEAD_SIZE)
    key_total_sum = key_portion.reshape(KEY_VALUE_HEADS, query_group_width, position_total, HEAD_SIZE).sum(axis=1)
    value_total_sum = value_portion.reshape(KEY_VALUE_HEADS, query_group_width, position_total, HEAD_SIZE).sum(axis=1)
    key_value_flat = jnp.stack([key_total_sum, value_total_sum], axis=1).transpose(2, 0, 1, 3).reshape(position_total, KEY_VALUE_HEADS * 2 * HEAD_SIZE)
    query_out = jnp.zeros((SEQUENCE_TOKENS, QUERY_HEADS * HEAD_SIZE), jnp.float32).at[token_row_set].add(jnp.where(filled_column, query_flat.astype(jnp.bfloat16).astype(jnp.float32), 0.0))
    key_value_output = jnp.zeros((SEQUENCE_TOKENS, KEY_VALUE_HEADS * 2 * HEAD_SIZE), jnp.float32).at[token_row_set].add(jnp.where(filled_column, key_value_flat.astype(jnp.bfloat16).astype(jnp.float32), 0.0))
    proj_out = jnp.dot(upstream_kept.T, attn_flat, preferred_element_type=jnp.float32)
    return (query_out.astype(jnp.bfloat16), key_value_output.astype(jnp.bfloat16), proj_out.astype(jnp.bfloat16))
```

```python
import functools
import math

import jax
import jax.numpy as jnp
from jax import lax
from jax.experimental import pallas as pl
from jax.experimental.pallas import tpu as pltpu
from jax.sharding import PartitionSpec as P

MESH = pl.DeviceIdType.MESH
BF = jnp.bfloat16
F32 = jnp.float32
NEG = -1e30
HEAD = 128
HEADS = 4
SLOTS = 192
ROWS = SLOTS + 16
PAIR = 2 * SLOTS
QROWS = HEADS * SLOTS
TOKENS = 256
NZ = 8
NX = 4
CHUNK = 256
SCALE = 1.0 / math.sqrt(HEAD)
LOG2 = SCALE * math.log2(math.e)
NT = (((1,), (1,)), ((), ()))


def mm(a, b):
    return jnp.dot(a, b, preferred_element_type=F32)


def kernel(
    keep_ref, q_ref, kv_ref, up_ref, w_ref,
    qo_ref, kvo_ref, po_ref,
    kvb, wb, ub, eb, mb, qr, dor, ot, dqt, stat, pickt, attn, doacc,
    pj, pjs, pjy, pjr, dkv, sib, rrx, yrx,
    kv_rs, kv_ss, kvsib_rs, kvsib_ss, kvy_ss,
    w_rs, w_ss, wsib_rs, wsib_ss, wy_rs, wy_ss, wys_rs, wys_ss,
    u_rs, u_ss,
    pjs_rs, pjs_ss, pjy_rs, pjy_ss, pjr_rs, pjr_ss,
    sib_rs, sib_ss, rrx_rs, rrx_ss, yrx_s,
):
    ctx = lax.axis_index("ctx")
    tp = lax.axis_index("tp")
    y = ctx // (2 * NZ)
    z = (ctx // 2) % NZ
    k = ctx % 2
    yh = tp // NX
    x = tp % NX

    def at_z(zz):
        return y * 2 * NZ + (zz % NZ) * 2 + k

    ring = ((at_z(z + 1), tp), (at_z(z + NZ - 1), tp))
    sibling = (ctx + 1 - 2 * k, tp)
    across = ((1 - y) * 2 * NZ + z * 2 + k, tp)
    xring = ((ctx, yh * NX + (x + 1) % NX), (ctx, yh * NX + (x + NX - 1) % NX))
    yh_peer = (ctx, (1 - yh) * NX + x)
    upper = y == 1
    lower = y == 0

    barrier = pltpu.get_barrier_semaphore()
    peers = ring + (sibling, across) + xring + (yh_peer,)
    for peer in peers:
        pl.semaphore_signal(barrier, inc=1, device_id=peer, device_id_type=MESH)

    pending = []

    def copy(src, dst, ssem, rsem, dev):
        return pltpu.make_async_remote_copy(
            src_ref=src, dst_ref=dst, send_sem=ssem, recv_sem=rsem,
            device_id=dev, device_id_type=MESH,
        )

    def send(cond, make):
        pending.append((cond, make))
        make().start()

    def got(ref, sem):
        copy(ref, ref, sem, sem, sibling).wait_recv()

    keep = keep_ref[...]
    pick_t = jnp.where(
        lax.broadcasted_iota(jnp.int32, (TOKENS, TOKENS), 0) == keep, 1.0, 0.0
    ).astype(F32)
    pickt[...] = pick_t.astype(BF)
    pick = pick_t.T.astype(BF)[:SLOTS]
    count = jnp.sum(jnp.where(keep >= 0, 1.0, 0.0), axis=1, keepdims=True)
    kvb[ctx, 0:SLOTS, :] = mm(pick, kv_ref[...]).astype(BF)
    kvb[ctx, SLOTS:ROWS, :] = jnp.broadcast_to(count, (ROWS - SLOTS, 2 * HEAD)).astype(BF)
    wb[ctx] = w_ref[...]
    ub[tp] = mm(pick, up_ref[...]).astype(BF)
    q_kept = mm(pick, q_ref[...]).astype(BF)
    for h in range(HEADS):
        qr[h * SLOTS:(h + 1) * SLOTS, :] = q_kept[:, h * HEAD:(h + 1) * HEAD]

    pl.semaphore_wait(barrier, len(peers))

    def slot_of(row, side, dist):
        zz = (z + NZ - dist) % NZ if side == 0 else (z + dist) % NZ
        return row * 2 * NZ + zz * 2 + k

    def kv_part(slot, side, dist):
        if dist < 4:
            return kvb.at[slot]
        return kvb.at[slot, pl.ds(0, 112)] if side == 0 else kvb.at[slot, pl.ds(112, 96)]

    def w_part(slot, side, dist):
        if dist < 4:
            return wb.at[slot]
        return wb.at[slot, pl.ds(side * 64, 64)]

    rows_of = (y, 0)

    def kv_ring(q, side, dist, cond=None):
        part = lambda: kv_part(slot_of(rows_of[q], side, dist), side, dist + 1)
        send(cond, lambda: copy(
            part(), part(), kv_ss.at[q, side, dist], kv_rs.at[q, side, dist + 1], ring[side]))

    def kv_sib(q, side, dist, cond=None):
        part = lambda: kv_part(slot_of(rows_of[q], side, dist), side, dist)
        send(cond, lambda: copy(
            part(), part(), kvsib_ss.at[q, side, dist], kvsib_rs.at[q, side, dist], sibling))

    def kv_sib_got(q, side, dist):
        slot = slot_of(rows_of[q], side, dist) + 1 - 2 * k
        got(kv_part(slot, side, dist), kvsib_rs.at[q, side, dist])

    def w_ring(side, dist):
        part = lambda: w_part(slot_of(y, side, dist), side, dist + 1)
        send(None, lambda: copy(
            part(), part(), w_ss.at[side, dist], w_rs.at[side, dist + 1], ring[side]))

    def w_out(side, dist):
        part = lambda: w_part(slot_of(y, side, dist), side, dist)
        send(None, lambda: copy(
            part(), part(), wy_ss.at[side, dist], wy_rs.at[side, dist], across))
        send(None, lambda: copy(
            part(), part(), wsib_ss.at[side, dist], wsib_rs.at[side, dist], sibling))

    def w_across(side, dist):
        part = lambda: w_part(slot_of(1 - y, side, dist), side, dist)
        got(part(), wy_rs.at[side, dist])
        send(None, lambda: copy(
            part(), part(), wys_ss.at[side, dist], wys_rs.at[side, dist], sibling))

    def w_sib_got(side, dist):
        turn = 1 - 2 * k
        got(w_part(slot_of(y, side, dist) + turn, side, dist), wsib_rs.at[side, dist])
        got(w_part(slot_of(1 - y, side, dist) + turn, side, dist), wys_rs.at[side, dist])

    def u_slot(h, side, dist):
        xx = (x + NX - dist) % NX if side == 0 else (x + dist) % NX
        return (yh if h == 0 else 1 - yh) * NX + xx

    def u_part(h, side, dist, half):
        slot = u_slot(h, side, dist)
        return ub.at[slot, pl.ds(side * 96, 96)] if half else ub.at[slot]

    def u_ring(h, side, dist):
        part = lambda: u_part(h, side, dist, dist + 1 == 2)
        send(None, lambda: copy(
            part(), part(), u_ss.at[h, side, dist], u_rs.at[h, side, dist + 1], xring[side]))

    def u_got(h, side, dist):
        got(u_part(h, side, dist, dist == 2), u_rs.at[h, side, dist])

    for side in (0, 1):
        kv_ring(0, side, 0)

    @pl.when(lower)
    def _():
        send(lower, lambda: copy(
            kvb.at[ctx], kvb.at[ctx], kvy_ss.at[0], kv_rs.at[1, 0, 0], across))

    kv_sib(0, 0, 0)
    for side in (0, 1):
        w_ring(side, 0)
    w_out(0, 0)
    for side in (0, 1):
        u_ring(0, side, 0)
    send(None, lambda: copy(ub.at[tp], ub.at[tp], u_ss.at[0, 0, 2], u_rs.at[1, 0, 0], yh_peer))

    ot[...] = jnp.zeros_like(ot)
    dqt[...] = jnp.zeros_like(dqt)
    stat[0:1, :] = jnp.full((1, QROWS), NEG, F32)
    stat[1:2, :] = jnp.zeros((1, QROWS), F32)

    def load_pair(p):
        block = kvb[pl.ds(2 * p, 2), 0:SLOTS, :]
        return (block[:, :, 0:HEAD].reshape(PAIR, HEAD), block[:, :, HEAD:].reshape(PAIR, HEAD))

    def turned(block):
        return block.astype(F32).T.astype(BF)

    def forward_block(p, own):
        keys, values = load_pair(p)
        values_t = turned(values)
        counts = kvb[pl.ds(2 * p, 2), SLOTS:ROWS, 0:HEAD].astype(F32)
        place = lax.broadcasted_iota(jnp.int32, (SLOTS, HEAD), 0).astype(F32)
        bias = jnp.concatenate(
            [jnp.where(place < counts[i, 0:1, :], 0.0, NEG) for i in (0, 1)], axis=0)
        bias = jnp.concatenate([bias] * (CHUNK // HEAD), axis=1)
        for first in range(0, QROWS, CHUNK):
            cols = slice(first, first + CHUNK)
            scores = lax.dot_general(keys, qr[cols, :], NT, preferred_element_type=F32) + bias
            if own:
                row = lax.broadcasted_iota(jnp.int32, (SLOTS, CHUNK), 0)
                col = (lax.broadcasted_iota(jnp.int32, (SLOTS, CHUNK), 1) + first) % SLOTS
                late = jnp.concatenate(
                    [jnp.where(row - col <= (k - i) * 1024, 0.0, NEG) for i in (0, 1)], axis=0)
                scores = scores + late
            old = stat[0:1, cols]
            new = jnp.maximum(old, jnp.max(scores, axis=0, keepdims=True) * LOG2)
            weights = jnp.exp2(scores * LOG2 - new)
            shrink = jnp.exp2(old - new)
            stat[0:1, cols] = new
            stat[1:2, cols] = stat[1:2, cols] * shrink + jnp.sum(weights, axis=0, keepdims=True)
            half = weights.astype(BF)
            eb[p, :, cols] = half
            mb[p, 0:1, cols] = new
            ot[:, cols] = ot[:, cols] * shrink + mm(values_t, half)

    kv_sib_got(0, 0, 0)
    forward_block(y * NZ + z, True)

    @pl.when(upper)
    def _():
        got(kvb.at[slot_of(0, 0, 0)], kv_rs.at[1, 0, 0])
        for side in (0, 1):
            kv_ring(1, side, 0, upper)
        kv_sib(1, 0, 0, upper)

    def forward_at(dist):
        sides = (0, 1) if 0 < dist < 4 else (0,)
        halves = (0, 1) if dist > 0 else (0,)
        if dist > 0:
            for side in halves:
                kv_sib_got(0, side, dist)

        @pl.when(upper)
        def _():
            for side in halves:
                kv_sib_got(1, side, dist)

        def step(i, carry):
            q = i // len(sides)
            side = i % len(sides)
            shift = jnp.where(side == 0, NZ - dist, dist)
            zz = (z + shift) % NZ
            needed = jnp.logical_or(
                jnp.logical_and(q == 0, zz < z), jnp.logical_and(q == 1, upper))

            @pl.when(needed)
            def _():
                forward_block(jnp.where(q == 0, y * NZ, 0) + zz, False)

            return carry

        lax.fori_loop(0, 2 * len(sides), step, 0)

    for dist in range(1, 5):
        for side in (0, 1):
            got(kv_part(slot_of(y, side, dist), side, dist), kv_rs.at[0, side, dist])
            if dist < 4:
                kv_ring(0, side, dist)
            kv_sib(0, side, dist)
        for side in (0, 1):
            got(w_part(slot_of(y, side, dist), side, dist), w_rs.at[side, dist])
            if dist < 4:
                w_ring(side, dist)
            w_out(side, dist)

        @pl.when(upper)
        def _():
            for side in (0, 1):
                got(kv_part(slot_of(0, side, dist), side, dist), kv_rs.at[1, side, dist])
                if dist < 4:
                    kv_ring(1, side, dist, upper)
                kv_sib(1, side, dist, upper)

        if dist == 1:
            for side in (0, 1):
                u_got(0, side, 1)
                u_ring(0, side, 1)
            got(ub.at[u_slot(1, 0, 0)], u_rs.at[1, 0, 0])
            for side in (0, 1):
                u_ring(1, side, 0)
        if dist == 2:
            for side in (0, 1):
                u_got(1, side, 1)
                u_ring(1, side, 1)
        forward_at(dist - 1)
        for side in ((0, 1) if dist > 1 else (0,)):
            w_across(side, dist - 1)
    forward_at(4)

    total = stat[1:2, :]
    inv = 1.0 / total
    stat[1:2, :] = inv
    attn_t = (ot[...] * inv).astype(BF).astype(F32)
    ot[...] = attn_t
    attn_rows = attn_t.T.astype(BF)
    for h in range(HEADS):
        attn[0:SLOTS, h * HEAD:(h + 1) * HEAD] = attn_rows[h * SLOTS:(h + 1) * SLOTS, :]
    attn[SLOTS:, :] = jnp.zeros((TOKENS - SLOTS, HEADS * HEAD), BF)

    for h in (0, 1):
        for side in (0, 1):
            u_got(h, side, 2)

    def proj_terms(i, carry):
        block = jnp.concatenate(
            [ub[i].astype(F32), jnp.zeros((TOKENS - SLOTS, HEADS * HEAD), F32)], axis=0)
        term = mm(block.T.astype(BF), attn[...]).astype(BF)
        pj[pl.ds(4 * i, 4)] = term.reshape(4, 128, HEADS * HEAD)
        return carry

    lax.fori_loop(0, 8, proj_terms, 0)

    def pj_slot(row, j, core):
        return row * 2 * NZ + ((z + j) % NZ) * 2 + core

    order = (4, 3, 5, 2, 6, 1, 7, 0)
    for turn in (1, 0):
        row = y if turn == 0 else 1 - y
        for j in order:
            def make(row=row, j=j, turn=turn):
                return copy(pj.at[pj_slot(row, j, 1 - k)], pjs.at[turn, j],
                            pjs_ss.at[turn, j], pjs_rs.at[turn, j], sibling)
            send(None, make)

    for side in (0, 1):
        w_across(side, 4)
    for dist in range(0, 5):
        for side in ((0, 1) if dist > 0 else (0,)):
            w_sib_got(side, dist)

    doacc[...] = jnp.zeros_like(doacc)

    def head_grads(i, carry):
        doacc[...] += mm(ub[i], wb[pl.ds(4 * i, 4)].reshape(4 * 128, HEADS * HEAD))
        return carry

    lax.fori_loop(0, 8, head_grads, 0)
    for h in range(HEADS):
        grads = doacc[:, h * HEAD:(h + 1) * HEAD].astype(BF)
        dor[h * SLOTS:(h + 1) * SLOTS, :] = grads
    stat[2:3, :] = jnp.sum(dor[...].astype(F32).T * ot[...], axis=0, keepdims=True)

    for j in order:
        got(pjs.at[1, j], pjs_rs.at[1, j])
        slot = pj_slot(1 - y, j, k)
        pj[slot] = (pj[slot].astype(F32) + pjs[1, j].astype(F32)).astype(BF)

        def make(j=j):
            return copy(pj.at[pj_slot(1 - y, j, k)], pjy.at[j],
                        pjy_ss.at[j], pjy_rs.at[j], across)
        send(None, make)

    def backward_block(p, q, j):
        keys, values = load_pair(p)
        keys_t = turned(keys)
        key_grad = jnp.zeros((PAIR, HEAD), F32)
        value_grad = jnp.zeros((PAIR, HEAD), F32)
        for first in range(0, QROWS, CHUNK):
            cols = slice(first, first + CHUNK)
            level = jnp.exp2(mb[p, 0:1, cols] - stat[0:1, cols]) * stat[1:2, cols]
            probs = eb[p, :, cols].astype(F32) * level
            grads = dor[cols, :]
            value_grad = value_grad + mm(probs.astype(BF), grads)
            pushes = lax.dot_general(values, grads, NT, preferred_element_type=F32)
            slopes = (probs * (pushes - stat[2:3, cols])).astype(BF)
            key_grad = key_grad + mm(slopes, qr[cols, :])
            dqt[:, cols] += mm(keys_t, slopes)
        dkv[q, j, :, :, 0:HEAD] = (key_grad * SCALE).astype(BF).reshape(2, SLOTS, HEAD)
        dkv[q, j, :, :, HEAD:] = value_grad.astype(BF).reshape(2, SLOTS, HEAD)

    def sides_of(dist):
        return (0, 1) if 0 < dist < 4 else (0,)

    def j_of(side, dist):
        return dist if side == 0 else NZ - dist

    def backward_at(dist):
        sides = sides_of(dist)

        def step(i, carry):
            q = i // len(sides)
            side = i % len(sides)
            j = jnp.where(side == 0, dist, NZ - dist)
            zz = (z + j) % NZ
            needed = jnp.logical_or(
                jnp.logical_and(q == 0, zz <= z), jnp.logical_and(q == 1, upper))

            @pl.when(needed)
            def _():
                backward_block(jnp.where(q == 0, y * NZ, 0) + zz, q, j)

            @pl.when(jnp.logical_not(needed))
            def _():
                dkv[q, j] = jnp.zeros((2, SLOTS, 2 * HEAD), BF)

            return carry

        lax.fori_loop(0, 2 * len(sides), step, 0)

        def swap(q, cond):
            for side in sides:
                j = j_of(side, dist)
                send(cond, lambda j=j: copy(
                    dkv.at[q, j, 1 - k], sib.at[q, j], sib_ss.at[q, j], sib_rs.at[q, j], sibling))

        swap(0, None)

        @pl.when(upper)
        def _():
            swap(1, upper)

    def add_into(ref, parts):
        value = ref[...].astype(F32)
        for part in parts:
            value = value + part[...].astype(F32)
        ref[...] = value.astype(BF)

    def kv_pass(dist, q, cond):
        for side in sides_of(dist):
            j = j_of(side, dist)
            got(sib.at[q, j], sib_rs.at[q, j])
            add_into(dkv.at[q, j, k], [sib.at[q, j]])
            if dist == 3:
                half = pl.ds(side * 96, 96)
                got(rrx.at[q, side, 3, half], rrx_rs.at[q, side, 3])
                add_into(dkv.at[q, j, k, half], [rrx.at[q, side, 3, half]])
            elif dist < 3:
                got(rrx.at[q, side, dist], rrx_rs.at[q, side, dist])
                add_into(dkv.at[q, j, k], [rrx.at[q, side, dist]])
        if dist == 0:
            got(rrx.at[q, 1, 0], rrx_rs.at[q, 1, 0])
            add_into(dkv.at[q, 0, k], [rrx.at[q, 1, 0]])
            return
        for side in (0, 1):
            j = j_of(side, dist)

            def make(j=j, side=side):
                if dist == 4:
                    half = pl.ds(side * 96, 96)
                    src, dst = dkv.at[q, 4, k, half], rrx.at[q, side, 3, half]
                else:
                    src, dst = dkv.at[q, j, k], rrx.at[q, side, dist - 1]
                return copy(src, dst, rrx_ss.at[q, side, dist - 1],
                            rrx_rs.at[q, side, dist - 1], ring[side])
            send(cond, make)

    def proj_pass(dist):
        for side in sides_of(dist):
            j = j_of(side, dist)
            slot = pj_slot(y, j, k)
            got(pjs.at[0, j], pjs_rs.at[0, j])
            got(pjy.at[j], pjy_rs.at[j])
            add_into(pj.at[slot], [pjs.at[0, j], pjy.at[j]])
            if dist == 3:
                half = pl.ds(side * 64, 64)
                got(pjr.at[side, 3, half], pjr_rs.at[side, 3])
                add_into(pj.at[slot, half], [pjr.at[side, 3, half]])
            elif dist < 3:
                got(pjr.at[side, dist], pjr_rs.at[side, dist])
                add_into(pj.at[slot], [pjr.at[side, dist]])
        if dist == 0:
            got(pjr.at[1, 0], pjr_rs.at[1, 0])
            add_into(pj.at[pj_slot(y, 0, k)], [pjr.at[1, 0]])
            return
        for side in (0, 1):
            j = j_of(side, dist)

            def make(j=j, side=side):
                if dist == 4:
                    half = pl.ds(side * 64, 64)
                    src, dst = pj.at[pj_slot(y, 4, k), half], pjr.at[side, 3, half]
                else:
                    src, dst = pj.at[pj_slot(y, j, k)], pjr.at[side, dist - 1]
                return copy(src, dst, pjr_ss.at[side, dist - 1],
                            pjr_rs.at[side, dist - 1], ring[side])
            send(None, make)

    def pass_on(dist):
        kv_pass(dist, 0, None)

        @pl.when(upper)
        def _():
            kv_pass(dist, 1, upper)

        proj_pass(dist)

    for dist in (4, 3, 2, 1, 0):
        backward_at(dist)
        if dist < 4:
            pass_on(dist + 1)

    query_rows = (dqt[...] * SCALE).T.astype(BF)
    empty = jnp.zeros((TOKENS - SLOTS, HEAD), BF)
    for h in range(HEADS):
        part = jnp.concatenate([query_rows[h * SLOTS:(h + 1) * SLOTS, :], empty], axis=0)
        qo_ref[:, h * HEAD:(h + 1) * HEAD] = mm(pickt[...], part).astype(BF)

    @pl.when(upper)
    def _():
        kv_pass(0, 1, upper)
        send(upper, lambda: copy(dkv.at[1, 0, k], yrx, yrx_s.at[0], yrx_s.at[1], across))

    kv_pass(0, 0, None)
    proj_pass(0)
    po_ref[...] = pj[pj_slot(y, 0, k)]

    @pl.when(lower)
    def _():
        got(yrx, yrx_s.at[1])
        add_into(dkv.at[0, 0, k], [yrx])

    sums = jnp.concatenate(
        [dkv[0, 0, k], jnp.zeros((TOKENS - SLOTS, 2 * HEAD), BF)], axis=0)
    kvo_ref[...] = mm(pickt[...], sums).astype(BF)

    for cond, make in pending:
        if cond is None:
            make().wait_send()
        else:
            @pl.when(cond)
            def _():
                make().wait_send()


def shards(queries, keys_values, upstream, out_proj, keep_index):
    keep = jnp.pad(keep_index, (0, TOKENS - SLOTS), constant_values=-1).reshape(1, TOKENS)
    dma = pltpu.SemaphoreType.DMA
    width = HEADS * HEAD
    vmem = pltpu.VMEM
    scratch = [
        vmem((4 * NZ, ROWS, 2 * HEAD), BF),
        vmem((4 * NZ, 128, width), BF),
        vmem((2 * NX, SLOTS, width), BF),
        vmem((2 * NZ, PAIR, QROWS), BF),
        vmem((2 * NZ, 8, QROWS), F32),
        vmem((QROWS, HEAD), BF),
        vmem((QROWS, HEAD), BF),
        vmem((HEAD, QROWS), F32),
        vmem((HEAD, QROWS), F32),
        vmem((8, QROWS), F32),
        vmem((TOKENS, TOKENS), BF),
        vmem((TOKENS, width), BF),
        vmem((SLOTS, width), F32),
        vmem((4 * NZ, 128, width), BF),
        vmem((2, NZ, 128, width), BF),
        vmem((NZ, 128, width), BF),
        vmem((2, 4, 128, width), BF),
        vmem((2, NZ, 2, SLOTS, 2 * HEAD), BF),
        vmem((2, NZ, SLOTS, 2 * HEAD), BF),
        vmem((2, 2, 4, SLOTS, 2 * HEAD), BF),
        vmem((SLOTS, 2 * HEAD), BF),
        dma((2, 2, 5)), dma((2, 2, 5)), dma((2, 2, 5)), dma((2, 2, 5)), dma((1,)),
        dma((2, 5)), dma((2, 5)), dma((2, 5)), dma((2, 5)),
        dma((2, 5)), dma((2, 5)), dma((2, 5)), dma((2, 5)),
        dma((2, 2, 3)), dma((2, 2, 3)),
        dma((2, NZ)), dma((2, NZ)), dma((NZ,)), dma((NZ,)), dma((2, 4)), dma((2, 4)),
        dma((2, NZ)), dma((2, NZ)), dma((2, 2, 4)), dma((2, 2, 4)), dma((2,)),
    ]
    return pl.pallas_call(
        kernel,
        out_shape=(
            jax.ShapeDtypeStruct(queries.shape, BF),
            jax.ShapeDtypeStruct(keys_values.shape, BF),
            jax.ShapeDtypeStruct(out_proj.shape, BF),
        ),
        in_specs=[pl.BlockSpec(memory_space=pltpu.VMEM)] * 5,
        out_specs=[pl.BlockSpec(memory_space=pltpu.VMEM)] * 3,
        scratch_shapes=scratch,
        compiler_params=pltpu.CompilerParams(
            collective_id=0, has_side_effects=True, vmem_limit_bytes=56 * 1024 * 1024
        ),
    )(keep, queries, keys_values, upstream, out_proj)


def solution(mesh):
    in_specs = (P("ctx", "tp"), P("ctx", "tp"), P("ctx", "tp"), P("ctx", "tp"), P("ctx"))
    out_specs = (P("ctx", "tp"), P("ctx", "tp"), P("ctx", "tp"))
    return jax.shard_map(shards, mesh=mesh, in_specs=in_specs, out_specs=out_specs, check_vma=False)
```

```python
import functools
import math

import jax
import jax.numpy as jnp
from jax import lax
from jax.experimental import pallas as pl
from jax.experimental.pallas import tpu as pltpu
from jax.sharding import PartitionSpec as P

MESH = pl.DeviceIdType.MESH
BF = jnp.bfloat16
F32 = jnp.float32
NEG = -1e30
HEAD = 128
HEADS = 4
SLOTS = 192
ROWS = SLOTS + 16
PAIR = 2 * SLOTS
QROWS = HEADS * SLOTS
TOKENS = 256
NZ = 8
NX = 4
CHUNK = 256
SCALE = 1.0 / math.sqrt(HEAD)
LOG2 = SCALE * math.log2(math.e)
NT = (((1,), (1,)), ((), ()))


def mm(a, b):
    return jnp.dot(a, b, preferred_element_type=F32)


def kernel(
    keep_ref, q_ref, kv_ref, up_ref, w_ref,
    qo_ref, kvo_ref, po_ref,
    kvb, wb, ub, uown, eb, mb, qr, dor, ot, dqt, stat, pickt, attn, doacc, dsend, drecv, keeps,
    pj, pjs, pjr, dkv, sib, rrx, yvx, ykx,
    kv_rs, kv_ss, kvsib_rs, kvsib_ss, kvy_ss, vy_rs, vy_ss, vsib_rs, vsib_ss,
    w_rs, w_ss, wsib_rs, wsib_ss,
    u_rs, u_ss, uo_ss, do_s, at_s,
    pjs_rs, pjs_ss, pjr_rs, pjr_ss,
    sib_rs, sib_ss, rrx_rs, rrx_ss, yv_rs, yv_ss, yk_s,
):
    ctx = lax.axis_index("ctx")
    tp = lax.axis_index("tp")
    y = ctx // (2 * NZ)
    z = (ctx // 2) % NZ
    k = ctx % 2
    yh = tp // NX
    x = tp % NX

    def at_z(zz):
        return y * 2 * NZ + (zz % NZ) * 2 + k

    ring = ((at_z(z + 1), tp), (at_z(z + NZ - 1), tp))
    sibling = (ctx + 1 - 2 * k, tp)
    across = ((1 - y) * 2 * NZ + z * 2 + k, tp)
    xring = ((ctx, yh * NX + (x + 1) % NX), (ctx, yh * NX + (x + NX - 1) % NX))
    yh_peer = (ctx, (1 - yh) * NX + x)
    diagonal = (across[0], yh_peer[1])
    upper = y == 1
    lower = y == 0
    aligned = y == yh
    crossed = y != yh

    barrier = pltpu.get_barrier_semaphore()
    peers = ring + (sibling, across) + xring + (yh_peer, diagonal)
    for peer in peers:
        pl.semaphore_signal(barrier, inc=1, device_id=peer, device_id_type=MESH)

    pending = []

    def copy(src, dst, ssem, rsem, dev):
        return pltpu.make_async_remote_copy(
            src_ref=src, dst_ref=dst, send_sem=ssem, recv_sem=rsem,
            device_id=dev, device_id_type=MESH,
        )

    def send(cond, make):
        pending.append((cond, make))
        make().start()

    def got(ref, sem):
        copy(ref, ref, sem, sem, sibling).wait_recv()

    keeps[0:1, :] = jnp.full((1, TOKENS), -1, jnp.int32)
    keeps[0:1, 0:SLOTS] = keep_ref[...]
    keep = keeps[0:1, :]
    pick_t = jnp.where(
        lax.broadcasted_iota(jnp.int32, (TOKENS, TOKENS), 0) == keep, 1.0, 0.0
    ).astype(F32)
    pickt[...] = pick_t.astype(BF)
    pick = pick_t.T.astype(BF)[:SLOTS]
    count = jnp.sum(jnp.where(keep >= 0, 1.0, 0.0), axis=1, keepdims=True)
    kvb[ctx, 0:SLOTS, :] = mm(pick, kv_ref[...]).astype(BF)
    kvb[ctx, SLOTS:ROWS, :] = jnp.broadcast_to(count, (ROWS - SLOTS, 2 * HEAD)).astype(BF)
    wb[ctx % (2 * NZ)] = w_ref[...]
    uown[...] = mm(pick, up_ref[...]).astype(BF)

    @pl.when(aligned)
    def _():
        ub[x, 0] = uown[...]

    q_kept = mm(pick, q_ref[...]).astype(BF)
    for h in range(HEADS):
        qr[h * SLOTS:(h + 1) * SLOTS, :] = q_kept[:, h * HEAD:(h + 1) * HEAD]

    pl.semaphore_wait(barrier, len(peers))

    def slot_of(row, side, dist):
        zz = (z + NZ - dist) % NZ if side == 0 else (z + dist) % NZ
        return row * 2 * NZ + zz * 2 + k

    def kv_part(slot, side, dist, cols):
        if dist < 4:
            rows = pl.ds(0, ROWS)
        else:
            rows = pl.ds(0, 112) if side == 0 else pl.ds(112, 96)
        return kvb.at[slot, rows, cols]

    ALL, KEY, VALUE = pl.ds(0, 2 * HEAD), pl.ds(0, HEAD), pl.ds(HEAD, HEAD)

    def w_part(slot, side, dist):
        if dist < 4:
            return wb.at[slot]
        return wb.at[slot, pl.ds(side * 64, 64)]

    rows_of = (y, 0)
    cols_of = (ALL, KEY)

    def kv_ring(q, side, dist, cond=None):
        part = lambda: kv_part(slot_of(rows_of[q], side, dist), side, dist + 1, cols_of[q])
        send(cond, lambda: copy(
            part(), part(), kv_ss.at[q, side, dist], kv_rs.at[q, side, dist + 1], ring[side]))

    def kv_sib(q, side, dist, cond=None):
        part = lambda: kv_part(slot_of(rows_of[q], side, dist), side, dist, cols_of[q])
        send(cond, lambda: copy(
            part(), part(), kvsib_ss.at[q, side, dist], kvsib_rs.at[q, side, dist], sibling))

    def kv_sib_got(q, side, dist):
        slot = slot_of(rows_of[q], side, dist) + 1 - 2 * k
        got(kv_part(slot, side, dist, cols_of[q]), kvsib_rs.at[q, side, dist])

    def v_out(side, dist):
        part = lambda: kv_part(slot_of(0, side, dist), side, dist, VALUE)
        send(lower, lambda: copy(
            part(), part(), vy_ss.at[side, dist], vy_rs.at[side, dist], across))

    def v_across(side, dist):
        part = lambda: kv_part(slot_of(0, side, dist), side, dist, VALUE)
        got(part(), vy_rs.at[side, dist])
        send(upper, lambda: copy(
            part(), part(), vsib_ss.at[side, dist], vsib_rs.at[side, dist], sibling))

    def v_sib_got(side, dist):
        got(kv_part(slot_of(0, side, dist) + 1 - 2 * k, side, dist, VALUE), vsib_rs.at[side, dist])

    def w_ring(side, dist):
        part = lambda: w_part(slot_of(0, side, dist), side, dist + 1)
        send(None, lambda: copy(
            part(), part(), w_ss.at[side, dist], w_rs.at[side, dist + 1], ring[side]))

    def w_sib(side, dist):
        part = lambda: w_part(slot_of(0, side, dist), side, dist)
        send(None, lambda: copy(
            part(), part(), wsib_ss.at[side, dist], wsib_rs.at[side, dist], sibling))

    def w_sib_got(side, dist):
        got(w_part(slot_of(0, side, dist) + 1 - 2 * k, side, dist), wsib_rs.at[side, dist])

    def u_part(h, side, dist, half):
        xx = (x + NX - dist) % NX if side == 0 else (x + dist) % NX
        return ub.at[xx, h, pl.ds(side * 96, 96)] if half else ub.at[xx, h]

    def u_ring(h, side, dist):
        part = lambda: u_part(h, side, dist, dist + 1 == 2)
        send(None, lambda: copy(
            part(), part(), u_ss.at[h, side, dist], u_rs.at[h, side, dist + 1], xring[side]))

    def u_got(h, side, dist):
        got(u_part(h, side, dist, dist == 2), u_rs.at[h, side, dist])

    for side in (0, 1):
        w_ring(side, 0)
        kv_ring(0, side, 0)

    @pl.when(lower)
    def _():
        part = lambda: kvb.at[ctx, :, KEY]
        send(lower, lambda: copy(part(), part(), kvy_ss.at[0], kv_rs.at[1, 0, 0], across))
        v_out(0, 0)

    @pl.when(aligned)
    def _():
        send(aligned, lambda: copy(uown, ub.at[x, 0], uo_ss.at[0], u_rs.at[0, 0, 0], yh_peer))

    @pl.when(crossed)
    def _():
        send(crossed, lambda: copy(uown, ub.at[x, 1], uo_ss.at[0], u_rs.at[1, 0, 0], across))
        send(crossed, lambda: copy(uown, ub.at[x, 1], uo_ss.at[1], u_rs.at[1, 0, 0], diagonal))

    kv_sib(0, 0, 0)
    w_sib(0, 0)

    ot[...] = jnp.zeros_like(ot)
    dqt[...] = jnp.zeros_like(dqt)
    stat[0:1, :] = jnp.full((1, QROWS), NEG, F32)
    stat[1:2, :] = jnp.zeros((1, QROWS), F32)

    def load_pair(p):
        block = kvb[pl.ds(2 * p, 2), 0:SLOTS, :]
        return (block[:, :, 0:HEAD].reshape(PAIR, HEAD), block[:, :, HEAD:].reshape(PAIR, HEAD))

    def turned(block):
        return block.astype(F32).T.astype(BF)

    def forward_block(p, own):
        keys, values = load_pair(p)
        values_t = turned(values)
        counts = kvb[pl.ds(2 * p, 2), SLOTS:ROWS, 0:HEAD].astype(F32)
        place = lax.broadcasted_iota(jnp.int32, (SLOTS, HEAD), 0).astype(F32)
        bias = jnp.concatenate(
            [jnp.where(place < counts[i, 0:1, :], 0.0, NEG) for i in (0, 1)], axis=0)
        bias = jnp.concatenate([bias] * (CHUNK // HEAD), axis=1)
        for first in range(0, QROWS, CHUNK):
            cols = slice(first, first + CHUNK)
            scores = lax.dot_general(keys, qr[cols, :], NT, preferred_element_type=F32) + bias
            if own:
                row = lax.broadcasted_iota(jnp.int32, (SLOTS, CHUNK), 0)
                col = (lax.broadcasted_iota(jnp.int32, (SLOTS, CHUNK), 1) + first) % SLOTS
                late = jnp.concatenate(
                    [jnp.where(row - col <= (k - i) * 1024, 0.0, NEG) for i in (0, 1)], axis=0)
                scores = scores + late
            old = stat[0:1, cols]
            new = jnp.maximum(old, jnp.max(scores, axis=0, keepdims=True) * LOG2)
            weights = jnp.exp2(scores * LOG2 - new)
            shrink = jnp.exp2(old - new)
            stat[0:1, cols] = new
            stat[1:2, cols] = stat[1:2, cols] * shrink + jnp.sum(weights, axis=0, keepdims=True)
            half = weights.astype(BF)
            eb[p, :, cols] = half
            mb[p, 0:1, cols] = new
            ot[:, cols] = ot[:, cols] * shrink + mm(values_t, half)

    kv_sib_got(0, 0, 0)
    forward_block(y * NZ + z, True)

    @pl.when(upper)
    def _():
        got(kvb.at[slot_of(0, 0, 0), :, KEY], kv_rs.at[1, 0, 0])
        for side in (0, 1):
            kv_ring(1, side, 0, upper)
        kv_sib(1, 0, 0, upper)
        v_across(0, 0)

    @pl.when(crossed)
    def _():
        got(ub.at[x, 0], u_rs.at[0, 0, 0])

    for side in (0, 1):
        u_ring(0, side, 0)

    def forward_at(dist):
        sides = (0, 1) if 0 < dist < 4 else (0,)
        halves = (0, 1) if dist > 0 else (0,)

        @pl.when(upper)
        def _():
            for side in halves:
                if dist > 0:
                    v_across(side, dist)

        if dist > 0:
            for side in halves:
                kv_sib_got(0, side, dist)

        def blocks(q):
            def step(side, carry):
                zz = (z + jnp.where(side == 0, NZ - dist, dist)) % NZ
                if q == 1:
                    forward_block(zz, False)
                else:
                    @pl.when(zz < z)
                    def _():
                        forward_block(y * NZ + zz, False)
                return carry

            lax.fori_loop(0, len(sides), step, 0)

        if dist > 0:
            blocks(0)

        @pl.when(upper)
        def _():
            for side in halves:
                kv_sib_got(1, side, dist)
                v_sib_got(side, dist)
            blocks(1)

    for dist in range(1, 5):
        for side in (0, 1):
            got(w_part(slot_of(0, side, dist), side, dist), w_rs.at[side, dist])
            if dist < 4:
                w_ring(side, dist)
            w_sib(side, dist)
            got(kv_part(slot_of(y, side, dist), side, dist, ALL), kv_rs.at[0, side, dist])
            if dist < 4:
                kv_ring(0, side, dist)
            kv_sib(0, side, dist)

        @pl.when(lower)
        def _():
            for side in (0, 1):
                v_out(side, dist)

        @pl.when(upper)
        def _():
            for side in (0, 1):
                got(kv_part(slot_of(0, side, dist), side, dist, KEY), kv_rs.at[1, side, dist])
                if dist < 4:
                    kv_ring(1, side, dist, upper)
                kv_sib(1, side, dist, upper)

        if dist == 1:
            got(ub.at[x, 1], u_rs.at[1, 0, 0])
            for side in (0, 1):
                u_ring(1, side, 0)
            for side in (0, 1):
                u_got(0, side, 1)
                u_ring(0, side, 1)
        if dist == 2:
            for side in (0, 1):
                u_got(1, side, 1)
                u_ring(1, side, 1)
        forward_at(dist - 1)

    for h in (0, 1):
        for side in (0, 1):
            u_got(h, side, 2)
    for dist in range(0, 5):
        for side in ((0, 1) if dist > 0 else (0,)):
            w_sib_got(side, dist)
    doacc[...] = jnp.zeros_like(doacc)

    def head_grads(i, carry):
        doacc[...] += mm(ub[i].reshape(PAIR, HEADS * HEAD),
                         wb[pl.ds(4 * i, 4)].reshape(4 * 128, HEADS * HEAD))
        return carry

    lax.fori_loop(0, NX, head_grads, 0)
    dsend[...] = doacc[SLOTS:, :].astype(BF)
    send(None, lambda: copy(dsend, drecv, do_s.at[0], do_s.at[1], across))

    forward_at(4)

    total = stat[1:2, :]
    inv = 1.0 / total
    stat[1:2, :] = inv
    attn_t = (ot[...] * inv).astype(BF).astype(F32)
    ot[...] = attn_t
    attn_rows = attn_t.T.astype(BF)
    for h in range(HEADS):
        attn[0, :, h * HEAD:(h + 1) * HEAD] = attn_rows[h * SLOTS:(h + 1) * SLOTS, :]
    send(None, lambda: copy(attn.at[0], attn.at[1], at_s.at[0], at_s.at[1], across))

    got(drecv, do_s.at[1])
    for h in range(HEADS):
        cols = slice(h * HEAD, (h + 1) * HEAD)
        grads = (doacc[0:SLOTS, cols] + drecv[:, cols].astype(F32)).astype(BF)
        dor[h * SLOTS:(h + 1) * SLOTS, :] = grads
    stat[2:3, :] = jnp.sum(dor[...].astype(F32).T * ot[...], axis=0, keepdims=True)

    def pj_slot(j, core):
        return ((z + j) % NZ) * 2 + core

    def proj_terms():
        got(attn.at[1], at_s.at[1])

        def step(i, carry):
            block = ub[i].reshape(PAIR, HEADS * HEAD).astype(F32)
            term = mm(block.T.astype(BF), attn[...].reshape(PAIR, HEADS * HEAD)).astype(BF)
            pj[pl.ds(4 * i, 4)] = term.reshape(4, 128, HEADS * HEAD)
            return carry

        lax.fori_loop(0, NX, step, 0)
        for j in (4, 3, 5, 2, 6, 1, 7, 0):
            send(None, lambda j=j: copy(
                pj.at[pj_slot(j, 1 - k)], pjs.at[j], pjs_ss.at[j], pjs_rs.at[j], sibling))

    def backward_block(p, q, j):
        keys, values = load_pair(p)
        keys_t = turned(keys)
        key_grad = jnp.zeros((PAIR, HEAD), F32)
        value_grad = jnp.zeros((PAIR, HEAD), F32)
        for first in range(0, QROWS, CHUNK):
            cols = slice(first, first + CHUNK)
            level = jnp.exp2(mb[p, 0:1, cols] - stat[0:1, cols]) * stat[1:2, cols]
            probs = eb[p, :, cols].astype(F32) * level
            grads = dor[cols, :]
            value_grad = value_grad + mm(probs.astype(BF), grads)
            pushes = lax.dot_general(values, grads, NT, preferred_element_type=F32)
            slopes = (probs * (pushes - stat[2:3, cols])).astype(BF)
            key_grad = key_grad + mm(slopes, qr[cols, :])
            dqt[:, cols] += mm(keys_t, slopes)
        dkv[q, j, :, :, 0:HEAD] = (key_grad * SCALE).astype(BF).reshape(2, SLOTS, HEAD)
        dkv[q, j, :, :, HEAD:] = value_grad.astype(BF).reshape(2, SLOTS, HEAD)

    def sides_of(dist):
        return (0, 1) if 0 < dist < 4 else (0,)

    def j_of(side, dist):
        return dist if side == 0 else NZ - dist

    def backward_at(dist):
        sides = sides_of(dist)

        def blocks(q):
            def step(side, carry):
                j = jnp.where(side == 0, dist, (NZ - dist) % NZ)
                zz = (z + j) % NZ
                if q == 1:
                    backward_block(zz, q, j)
                else:
                    @pl.when(zz <= z)
                    def _():
                        backward_block(y * NZ + zz, q, j)

                    @pl.when(zz > z)
                    def _():
                        dkv[q, j] = jnp.zeros((2, SLOTS, 2 * HEAD), BF)
                return carry

            lax.fori_loop(0, len(sides), step, 0)

        def swap(q, cond):
            for side in sides:
                j = j_of(side, dist)
                send(cond, lambda j=j: copy(
                    dkv.at[q, j, 1 - k], sib.at[q, j], sib_ss.at[q, j], sib_rs.at[q, j], sibling))

        @pl.when(upper)
        def _():
            blocks(1)
            swap(1, upper)

        blocks(0)
        swap(0, None)

    def add_into(ref, parts):
        value = ref[...].astype(F32)
        for part in parts:
            value = value + part[...].astype(F32)
        ref[...] = value.astype(BF)

    def kv_pass(dist, q, cond):
        cols = cols_of[q]
        for side in sides_of(dist):
            j = j_of(side, dist)
            got(sib.at[q, j], sib_rs.at[q, j])
            add_into(dkv.at[q, j, k], [sib.at[q, j]])
            if q == 1:
                send(upper, lambda j=j: copy(
                    dkv.at[1, j, k, :, VALUE], yvx.at[j], yv_ss.at[j], yv_rs.at[j], across))
            else:
                @pl.when(lower)
                def _():
                    got(yvx.at[j], yv_rs.at[j])
                    add_into(dkv.at[0, j, k, :, VALUE], [yvx.at[j]])
            if dist == 3:
                half = pl.ds(side * 96, 96)
                part = rrx.at[q, side, 3, half, cols]
                got(part, rrx_rs.at[q, side, 3])
                add_into(dkv.at[q, j, k, half, cols], [part])
            elif dist < 3:
                part = rrx.at[q, side, dist, :, cols]
                got(part, rrx_rs.at[q, side, dist])
                add_into(dkv.at[q, j, k, :, cols], [part])
        if dist == 0:
            part = rrx.at[q, 1, 0, :, cols]
            got(part, rrx_rs.at[q, 1, 0])
            add_into(dkv.at[q, 0, k, :, cols], [part])
            return
        for side in (0, 1):
            def make(side=side):
                if dist == 4:
                    half = pl.ds(side * 96, 96)
                    src, dst = dkv.at[q, 4, k, half, cols], rrx.at[q, side, 3, half, cols]
                else:
                    src = dkv.at[q, j_of(side, dist), k, :, cols]
                    dst = rrx.at[q, side, dist - 1, :, cols]
                return copy(src, dst, rrx_ss.at[q, side, dist - 1],
                            rrx_rs.at[q, side, dist - 1], ring[side])
            send(cond, make)

    def proj_pass(dist):
        for side in sides_of(dist):
            j = j_of(side, dist)
            slot = pj_slot(j, k)
            got(pjs.at[j], pjs_rs.at[j])
            parts = [pjs.at[j]]
            if 0 < dist < 3:
                got(pjr.at[side, dist], pjr_rs.at[side, dist])
                parts.append(pjr.at[side, dist])
            elif dist == 0:
                for other in (0, 1):
                    got(pjr.at[other, 0], pjr_rs.at[other, 0])
                    parts.append(pjr.at[other, 0])
            add_into(pj.at[slot], parts)
            if dist == 3:
                half = pl.ds(side * 64, 64)
                got(pjr.at[side, 3, half], pjr_rs.at[side, 3])
                add_into(pj.at[slot, half], [pjr.at[side, 3, half]])
        if dist == 0:
            return
        for side in (0, 1):
            def make(side=side):
                if dist == 4:
                    half = pl.ds(side * 64, 64)
                    src, dst = pj.at[pj_slot(4, k), half], pjr.at[side, 3, half]
                else:
                    src, dst = pj.at[pj_slot(j_of(side, dist), k)], pjr.at[side, dist - 1]
                return copy(src, dst, pjr_ss.at[side, dist - 1],
                            pjr_rs.at[side, dist - 1], ring[side])
            send(None, make)

    def pass_on(dist):
        @pl.when(upper)
        def _():
            kv_pass(dist, 1, upper)

        proj_pass(dist)
        kv_pass(dist, 0, None)

    for dist in (4, 3, 2, 1, 0):
        backward_at(dist)
        if dist == 4:
            proj_terms()
        else:
            pass_on(dist + 1)

    query_rows = (dqt[...] * SCALE).T.astype(BF)
    empty = jnp.zeros((TOKENS - SLOTS, HEAD), BF)
    for h in range(HEADS):
        part = jnp.concatenate([query_rows[h * SLOTS:(h + 1) * SLOTS, :], empty], axis=0)
        qo_ref[:, h * HEAD:(h + 1) * HEAD] = mm(pickt[...], part).astype(BF)

    @pl.when(upper)
    def _():
        kv_pass(0, 1, upper)
        send(upper, lambda: copy(
            dkv.at[1, 0, k, :, KEY], ykx, yk_s.at[0], yk_s.at[1], across))

    proj_pass(0)
    po_ref[...] = pj[pj_slot(0, k)]
    kv_pass(0, 0, None)

    @pl.when(lower)
    def _():
        got(ykx, yk_s.at[1])
        add_into(dkv.at[0, 0, k, :, KEY], [ykx])

    sums = jnp.concatenate(
        [dkv[0, 0, k], jnp.zeros((TOKENS - SLOTS, 2 * HEAD), BF)], axis=0)
    kvo_ref[...] = mm(pickt[...], sums).astype(BF)

    for cond, make in pending:
        if cond is None:
            make().wait_send()
        else:
            @pl.when(cond)
            def _():
                make().wait_send()


def shards(queries, keys_values, upstream, out_proj, keep_index):
    keep = keep_index.reshape(1, SLOTS)
    dma = pltpu.SemaphoreType.DMA
    width = HEADS * HEAD
    vmem = pltpu.VMEM
    scratch = [
        vmem((4 * NZ, ROWS, 2 * HEAD), BF),
        vmem((2 * NZ, 128, width), BF),
        vmem((NX, 2, SLOTS, width), BF),
        vmem((SLOTS, width), BF),
        vmem((2 * NZ, PAIR, QROWS), BF),
        vmem((2 * NZ, 8, QROWS), F32),
        vmem((QROWS, HEAD), BF),
        vmem((QROWS, HEAD), BF),
        vmem((HEAD, QROWS), F32),
        vmem((HEAD, QROWS), F32),
        vmem((8, QROWS), F32),
        vmem((TOKENS, TOKENS), BF),
        vmem((2, SLOTS, width), BF),
        vmem((PAIR, width), F32),
        vmem((SLOTS, width), BF),
        vmem((SLOTS, width), BF),
        vmem((8, TOKENS), jnp.int32),
        vmem((2 * NZ, 128, width), BF),
        vmem((NZ, 128, width), BF),
        vmem((2, 4, 128, width), BF),
        vmem((2, NZ, 2, SLOTS, 2 * HEAD), BF),
        vmem((2, NZ, SLOTS, 2 * HEAD), BF),
        vmem((2, 2, 4, SLOTS, 2 * HEAD), BF),
        vmem((NZ, SLOTS, HEAD), BF),
        vmem((SLOTS, HEAD), BF),
        dma((2, 2, 5)), dma((2, 2, 5)), dma((2, 2, 5)), dma((2, 2, 5)), dma((1,)),
        dma((2, 5)), dma((2, 5)), dma((2, 5)), dma((2, 5)),
        dma((2, 5)), dma((2, 5)), dma((2, 5)), dma((2, 5)),
        dma((2, 2, 3)), dma((2, 2, 3)), dma((2,)), dma((2,)), dma((2,)),
        dma((NZ,)), dma((NZ,)), dma((2, 4)), dma((2, 4)),
        dma((2, NZ)), dma((2, NZ)), dma((2, 2, 4)), dma((2, 2, 4)),
        dma((NZ,)), dma((NZ,)), dma((2,)),
    ]
    return pl.pallas_call(
        kernel,
        out_shape=(
            jax.ShapeDtypeStruct(queries.shape, BF),
            jax.ShapeDtypeStruct(keys_values.shape, BF),
            jax.ShapeDtypeStruct(out_proj.shape, BF),
        ),
        in_specs=[pl.BlockSpec(memory_space=pltpu.VMEM)] * 5,
        out_specs=[pl.BlockSpec(memory_space=pltpu.VMEM)] * 3,
        scratch_shapes=scratch,
        compiler_params=pltpu.CompilerParams(
            collective_id=0, has_side_effects=True, vmem_limit_bytes=56 * 1024 * 1024
        ),
    )(keep, queries, keys_values, upstream, out_proj)


def solution(mesh):
    in_specs = (P("ctx", "tp"), P("ctx", "tp"), P("ctx", "tp"), P("ctx", "tp"), P("ctx"))
    out_specs = (P("ctx", "tp"), P("ctx", "tp"), P("ctx", "tp"))
    return jax.shard_map(shards, mesh=mesh, in_specs=in_specs, out_specs=out_specs, check_vma=False)
```

```python
import functools
import math

import jax
import jax.numpy as jnp
from jax import lax
from jax.experimental import pallas as pl
from jax.experimental.pallas import tpu as pltpu
from jax.sharding import PartitionSpec as P

MESH = pl.DeviceIdType.MESH
BF = jnp.bfloat16
F32 = jnp.float32
NEG = -1e30
HEAD = 128
HEADS = 4
SLOTS = 192
ROWS = SLOTS + 16
PAIR = 2 * SLOTS
QROWS = HEADS * SLOTS
TOKENS = 256
CHUNK = 256
NZ = 8
NX = 4
SCALE = 1.0 / math.sqrt(HEAD)
LOG2 = SCALE * math.log2(math.e)
NT = (((1,), (1,)), ((), ()))


def mm(a, b):
    return jnp.dot(a, b, preferred_element_type=F32)


def kernel(
    keep_ref, q_ref, kv_ref, up_ref, w_ref,
    qo_ref, kvo_ref, po_ref,
    kvb, wb, ub, uown, eb, mb, qr, dor, ot, dqt, stat, pickt, attn, doacc, dsend, drecv, keeps,
    pj, pjs, pjr, dkv, sib, rrx, yvx,
    kv_rs, kv_ss, kvsib_rs, kvsib_ss, vy_rs, vy_ss, vsib_rs, vsib_ss,
    w_rs, w_ss, wsib_rs, wsib_ss,
    u_rs, u_ss, uo_ss, do_s, at_s,
    pjs_rs, pjs_ss, pjr_rs, pjr_ss,
    sib_rs, sib_ss, rrx_rs, rrx_ss, yv_rs, yv_ss,
):
    ctx = lax.axis_index("ctx")
    tp = lax.axis_index("tp")
    y = ctx // (2 * NZ)
    z = (ctx // 2) % NZ
    k = ctx % 2
    yh = tp // NX
    x = tp % NX

    def at_z(zz):
        return y * 2 * NZ + (zz % NZ) * 2 + k

    ring = ((at_z(z + 1), tp), (at_z(z + NZ - 1), tp))
    sibling = (ctx + 1 - 2 * k, tp)
    across = ((1 - y) * 2 * NZ + z * 2 + k, tp)
    xring = ((ctx, yh * NX + (x + 1) % NX), (ctx, yh * NX + (x + NX - 1) % NX))
    yh_peer = (ctx, (1 - yh) * NX + x)
    diagonal = (across[0], yh_peer[1])
    upper = y == 1
    lower = y == 0
    aligned = y == yh
    crossed = y != yh

    barrier = pltpu.get_barrier_semaphore()
    peers = ring + (sibling, across) + xring + (yh_peer, diagonal)
    for peer in peers:
        pl.semaphore_signal(barrier, inc=1, device_id=peer, device_id_type=MESH)

    pending = []

    def copy(src, dst, ssem, rsem, dev):
        return pltpu.make_async_remote_copy(
            src_ref=src, dst_ref=dst, send_sem=ssem, recv_sem=rsem,
            device_id=dev, device_id_type=MESH,
        )

    def send(cond, make):
        pending.append((cond, make))
        make().start()

    def got(ref, sem):
        copy(ref, ref, sem, sem, sibling).wait_recv()

    keeps[0:1, :] = jnp.full((1, TOKENS), -1, jnp.int32)
    keeps[0:1, 0:SLOTS] = keep_ref[...]
    keep = keeps[0:1, :]
    pick_t = jnp.where(
        lax.broadcasted_iota(jnp.int32, (TOKENS, TOKENS), 0) == keep, 1.0, 0.0
    ).astype(F32)
    pickt[...] = pick_t.astype(BF)
    pick = pick_t.T.astype(BF)[:SLOTS]
    count = jnp.sum(jnp.where(keep >= 0, 1.0, 0.0), axis=1, keepdims=True)
    kvb[ctx, 0:SLOTS, :] = mm(pick, kv_ref[...]).astype(BF)
    kvb[ctx, SLOTS:ROWS, :] = jnp.broadcast_to(count, (ROWS - SLOTS, 2 * HEAD)).astype(BF)
    uown[...] = mm(pick, up_ref[...]).astype(BF)
    wb[ctx % (2 * NZ)] = w_ref[...]

    @pl.when(aligned)
    def _():
        ub[x, 0] = uown[...]

    pl.semaphore_wait(barrier, len(peers))

    def slot_of(row, side, dist):
        zz = (z + NZ - dist) % NZ if side == 0 else (z + dist) % NZ
        return row * 2 * NZ + zz * 2 + k

    def kv_part(slot, side, dist, cols):
        if dist < 4:
            rows = pl.ds(0, ROWS)
        else:
            rows = pl.ds(0, 112) if side == 0 else pl.ds(112, 96)
        return kvb.at[slot, rows, cols]

    ALL, KEY, VALUE = pl.ds(0, 2 * HEAD), pl.ds(0, HEAD), pl.ds(HEAD, HEAD)

    def w_part(slot, side, dist):
        if dist < 4:
            return wb.at[slot]
        return wb.at[slot, pl.ds(side * 64, 64)]

    rows_of = (y, 0)
    cols_of = (ALL, KEY)

    def kv_ring(q, side, dist, cond=None):
        part = lambda: kv_part(slot_of(rows_of[q], side, dist), side, dist + 1, cols_of[q])
        send(cond, lambda: copy(
            part(), part(), kv_ss.at[q, side, dist], kv_rs.at[q, side, dist + 1], ring[side]))

    def kv_sib(q, side, dist, cond=None):
        part = lambda: kv_part(slot_of(rows_of[q], side, dist), side, dist, cols_of[q])
        send(cond, lambda: copy(
            part(), part(), kvsib_ss.at[q, side, dist], kvsib_rs.at[q, side, dist], sibling))

    def kv_sib_got(q, side, dist):
        slot = slot_of(rows_of[q], side, dist) + 1 - 2 * k
        got(kv_part(slot, side, dist, cols_of[q]), kvsib_rs.at[q, side, dist])

    def across_cols(dist):
        return VALUE if dist == 1 else ALL

    def v_out(side, dist):
        part = lambda: kv_part(slot_of(0, side, dist), side, dist, across_cols(dist))
        send(lower, lambda: copy(
            part(), part(), vy_ss.at[side, dist], vy_rs.at[side, dist], across))

    def v_across(side, dist):
        part = lambda: kv_part(slot_of(0, side, dist), side, dist, across_cols(dist))
        got(part(), vy_rs.at[side, dist])
        send(upper, lambda: copy(
            part(), part(), vsib_ss.at[side, dist], vsib_rs.at[side, dist], sibling))

    def v_sib_got(side, dist):
        slot = slot_of(0, side, dist) + 1 - 2 * k
        got(kv_part(slot, side, dist, across_cols(dist)), vsib_rs.at[side, dist])

    def w_ring(side, dist):
        part = lambda: w_part(slot_of(0, side, dist), side, dist + 1)
        send(None, lambda: copy(
            part(), part(), w_ss.at[side, dist], w_rs.at[side, dist + 1], ring[side]))

    def w_sib(side, dist):
        part = lambda: w_part(slot_of(0, side, dist), side, dist)
        send(None, lambda: copy(
            part(), part(), wsib_ss.at[side, dist], wsib_rs.at[side, dist], sibling))

    def w_sib_got(side, dist):
        got(w_part(slot_of(0, side, dist) + 1 - 2 * k, side, dist), wsib_rs.at[side, dist])

    def u_part(h, side, dist, half):
        xx = (x + NX - dist) % NX if side == 0 else (x + dist) % NX
        return ub.at[xx, h, pl.ds(side * 96, 96)] if half else ub.at[xx, h]

    def u_ring(h, side, dist, cond=None):
        part = lambda: u_part(h, side, dist, dist + 1 == 2)
        send(cond, lambda: copy(
            part(), part(), u_ss.at[h, side, dist], u_rs.at[h, side, dist + 1], xring[side]))

    def u_got(h, side, dist):
        got(u_part(h, side, dist, dist == 2), u_rs.at[h, side, dist])

    for side in (0, 1):
        kv_ring(0, side, 0)

    @pl.when(aligned)
    def _():
        send(aligned, lambda: copy(uown, ub.at[x, 0], uo_ss.at[0], u_rs.at[0, 0, 0], yh_peer))

    @pl.when(crossed)
    def _():
        send(crossed, lambda: copy(uown, ub.at[x, 1], uo_ss.at[0], u_rs.at[1, 0, 0], across))
        send(crossed, lambda: copy(uown, ub.at[x, 1], uo_ss.at[1], u_rs.at[1, 0, 0], diagonal))

    @pl.when(aligned)
    def _():
        for side in (0, 1):
            u_ring(0, side, 0, aligned)

    kv_sib(0, 0, 0)

    @pl.when(lower)
    def _():
        v_out(0, 0)

    q_kept = mm(pick, q_ref[...]).astype(BF)
    for h in range(HEADS):
        qr[h * SLOTS:(h + 1) * SLOTS, :] = q_kept[:, h * HEAD:(h + 1) * HEAD]

    ot[...] = jnp.zeros_like(ot)
    dqt[...] = jnp.zeros_like(dqt)
    stat[0:1, :] = jnp.full((1, QROWS), NEG, F32)
    stat[1:2, :] = jnp.zeros((1, QROWS), F32)

    def load_pair(p):
        block = kvb[pl.ds(2 * p, 2), 0:SLOTS, :]
        return (block[:, :, 0:HEAD].reshape(PAIR, HEAD), block[:, :, HEAD:].reshape(PAIR, HEAD))

    def turned(block):
        return block.astype(F32).T.astype(BF)

    def key_bias(p):
        counts = kvb[pl.ds(2 * p, 2), SLOTS:ROWS, 0:HEAD].astype(F32)
        place = lax.broadcasted_iota(jnp.int32, (SLOTS, HEAD), 0).astype(F32)
        bias = jnp.concatenate(
            [jnp.where(place < counts[i, 0:1, :], 0.0, NEG) for i in (0, 1)], axis=0)
        return jnp.concatenate([bias] * (CHUNK // HEAD), axis=1)

    def forward_blocks(pairs, own=False):
        loaded = [load_pair(p) for p in pairs]
        biases = [key_bias(p) for p in pairs]
        values_t = jnp.concatenate([turned(values) for _, values in loaded], axis=1)
        values_t = jnp.concatenate(
            [values_t, jnp.ones((16, PAIR * len(pairs)), BF)], axis=0)
        old = stat[0:1, :]
        maxima, halves = [], []
        for first in range(0, QROWS, CHUNK):
            cols = slice(first, first + CHUNK)
            new = old[:, cols]
            scores = []
            for (keys, _), bias in zip(loaded, biases):
                part = lax.dot_general(keys, qr[cols, :], NT, preferred_element_type=F32)
                part = part * LOG2 + bias
                if own:
                    row = lax.broadcasted_iota(jnp.int32, (SLOTS, CHUNK), 0)
                    col = (lax.broadcasted_iota(jnp.int32, (SLOTS, CHUNK), 1) + first) % SLOTS
                    part = part + jnp.concatenate(
                        [jnp.where(row - col <= (k - i) * 1024, 0.0, NEG) for i in (0, 1)], axis=0)
                scores.append(part)
                new = jnp.maximum(new, jnp.max(part, axis=0, keepdims=True))
            weights = [jnp.exp2(part - new).astype(BF) for part in scores]
            for p, part in zip(pairs, weights):
                eb[p, :, cols] = part
                mb[p, 0:1, cols] = new
            halves.append(jnp.concatenate(weights, axis=0))
            maxima.append(new)
        new = jnp.concatenate(maxima, axis=1)
        shrink = jnp.exp2(old - new)
        sums = mm(values_t, jnp.concatenate(halves, axis=1))
        ot[...] = ot[...] * shrink + sums[0:HEAD]
        stat[0:1, :] = new
        stat[1:2, :] = stat[1:2, :] * shrink + sums[HEAD:HEAD + 1]

    kv_sib_got(0, 0, 0)
    forward_blocks([y * NZ + z], True)

    for side in (0, 1):
        w_ring(side, 0)
    w_sib(0, 0)

    def sides_of(dist):
        return (0, 1) if 0 < dist < 4 else (0,)

    def chip_at(j):
        return (z + j) % NZ

    def forward_own_row(dist):
        for side in (0, 1):
            kv_sib_got(0, side, dist)
        before, behind = y * NZ + chip_at(NZ - dist), y * NZ + chip_at(dist)
        near, far = z >= dist, z + dist >= NZ

        @pl.when(jnp.logical_and(near, far))
        def _():
            forward_blocks([before, behind])

        @pl.when(near != far)
        def _():
            forward_blocks([jnp.where(near, before, behind)])

    def forward_other_row(dist):
        @pl.when(upper)
        def _():
            for side in ((0, 1) if dist > 0 else (0,)):
                if dist == 1:
                    kv_sib_got(1, side, dist)
                v_sib_got(side, dist)
            forward_blocks([chip_at(NZ - dist), chip_at(dist)] if dist > 0 else [z])

    def forward_opposite():
        for side in (0, 1):
            kv_sib_got(0, side, 4)
        there = chip_at(4)

        @pl.when(upper)
        def _():
            for side in (0, 1):
                v_sib_got(side, 4)

        @pl.when(jnp.logical_and(upper, z >= 4))
        def _():
            forward_blocks([there, y * NZ + there])

        @pl.when(upper != (z >= 4))
        def _():
            forward_blocks([there])

    def other_row_got(dist):
        @pl.when(upper)
        def _():
            for side in ((0, 1) if dist > 0 else (0,)):
                if dist == 1:
                    got(kv_part(slot_of(0, side, 1), side, 1, KEY), kv_rs.at[1, side, 1])
                    kv_sib(1, side, 1, upper)
                v_across(side, dist)
            if dist == 0:
                for side in (0, 1):
                    kv_ring(1, side, 0, upper)

    def w_got(dist):
        for side in (0, 1):
            got(w_part(slot_of(0, side, dist), side, dist), w_rs.at[side, dist])
            if dist < 4:
                w_ring(side, dist)
            w_sib(side, dist)

    def own_row_got(dist):
        for side in (0, 1):
            got(kv_part(slot_of(y, side, dist), side, dist, ALL), kv_rs.at[0, side, dist])
            if dist < 4:
                kv_ring(0, side, dist)
            kv_sib(0, side, dist)

        @pl.when(lower)
        def _():
            for side in (0, 1):
                v_out(side, dist)

    def u_first_got():
        @pl.when(crossed)
        def _():
            got(ub.at[x, 0], u_rs.at[0, 0, 0])
            for side in (0, 1):
                u_ring(0, side, 0, crossed)

        got(ub.at[x, 1], u_rs.at[1, 0, 0])
        for side in (0, 1):
            u_ring(1, side, 0)

    def u_next_got(h):
        for side in (0, 1):
            u_got(h, side, 1)
            u_ring(h, side, 1)

    own_row_got(1)
    w_got(1)
    other_row_got(0)
    u_first_got()
    forward_own_row(1)
    own_row_got(2)
    w_got(2)
    other_row_got(1)
    forward_other_row(0)
    u_next_got(0)
    forward_own_row(2)
    own_row_got(3)
    w_got(3)
    other_row_got(2)
    u_next_got(1)
    forward_other_row(1)
    own_row_got(4)
    w_got(4)
    forward_own_row(3)
    other_row_got(3)
    forward_other_row(2)
    other_row_got(4)
    forward_other_row(3)
    forward_opposite()

    total = stat[1:2, :]
    inv = 1.0 / total
    stat[1:2, :] = inv
    attn_t = (ot[...] * inv).astype(BF).astype(F32)
    ot[...] = attn_t
    attn_rows = attn_t.T.astype(BF)
    for h in range(HEADS):
        attn[0, :, h * HEAD:(h + 1) * HEAD] = attn_rows[h * SLOTS:(h + 1) * SLOTS, :]
    send(None, lambda: copy(attn.at[0], attn.at[1], at_s.at[0], at_s.at[1], across))

    for h in (0, 1):
        for side in (0, 1):
            u_got(h, side, 2)
    for dist in range(0, 5):
        for side in ((0, 1) if dist > 0 else (0,)):
            w_sib_got(side, dist)

    def head_grads(h):
        doacc[h] = jnp.zeros((SLOTS, HEADS * HEAD), F32)

        def step(i, carry):
            doacc[h] += mm(ub[i, h], wb[pl.ds(4 * i, 4)].reshape(4 * 128, HEADS * HEAD))
            return carry

        lax.fori_loop(0, NX, step, 0)

    head_grads(1)
    dsend[...] = doacc[1].astype(BF)
    send(None, lambda: copy(dsend, drecv, do_s.at[0], do_s.at[1], across))
    head_grads(0)

    def pj_slot(j, core):
        return ((z + j) % NZ) * 2 + core

    def proj_swap(j):
        return copy(pj.at[pj_slot(j, 1 - k)], pjs.at[j], pjs_ss.at[j], pjs_rs.at[j], sibling)

    def proj_terms():
        got(attn.at[1], at_s.at[1])

        def step(i, carry):
            xx = (((z + NZ // 2) % NZ) // 2 + jnp.where(i < 2, i, 5 - i)) % NX
            block = ub[xx].reshape(PAIR, HEADS * HEAD).astype(F32)
            term = mm(block.T.astype(BF), attn[...].reshape(PAIR, HEADS * HEAD)).astype(BF)
            pj[pl.ds(4 * xx, 4)] = term.reshape(4, 128, HEADS * HEAD)
            for i in (0, 1):
                proj_swap((2 * xx + i + NZ - z) % NZ).start()
            return carry

        lax.fori_loop(0, NX, step, 0)
        for j in range(NZ):
            pending.append((None, lambda j=j: proj_swap(j)))

    def head_grads_done():
        got(drecv, do_s.at[1])
        for h in range(HEADS):
            cols = slice(h * HEAD, (h + 1) * HEAD)
            grads = (doacc[0, :, cols] + drecv[:, cols].astype(F32)).astype(BF)
            dor[h * SLOTS:(h + 1) * SLOTS, :] = grads
        stat[2:3, :] = jnp.sum(dor[...].astype(F32).T * ot[...], axis=0, keepdims=True)

    def backward_blocks(items):
        loaded = [load_pair(p) for p, _, _ in items]
        keys_t = jnp.concatenate([turned(keys) for keys, _ in loaded], axis=1)
        values = jnp.concatenate([values for _, values in loaded], axis=0)
        probs = jnp.concatenate([
            eb[p].astype(F32) * (jnp.exp2(mb[p, 0:1, :] - stat[0:1, :]) * stat[1:2, :])
            for p, _, _ in items], axis=0)
        grads = dor[...]
        value_grad = mm(probs.astype(BF), grads)
        pushes = lax.dot_general(values, grads, NT, preferred_element_type=F32)
        slopes = (probs * (pushes - stat[2:3, :])).astype(BF)
        key_grad = mm(slopes, qr[...])
        dqt[...] += mm(keys_t, slopes)
        for i, (_, q, j) in enumerate(items):
            rows = slice(i * PAIR, (i + 1) * PAIR)
            dkv[q, j, :, :, 0:HEAD] = (key_grad[rows] * SCALE).astype(BF).reshape(2, SLOTS, HEAD)
            dkv[q, j, :, :, HEAD:] = value_grad[rows].astype(BF).reshape(2, SLOTS, HEAD)

    def no_grads(j):
        dkv[0, j] = jnp.zeros((2, SLOTS, 2 * HEAD), BF)

    def j_of(side, dist):
        return dist if side == 0 else NZ - dist

    def swap_grads(dist, q):
        for side in sides_of(dist):
            j = j_of(side, dist)
            send(upper if q else None, lambda j=j: copy(
                dkv.at[q, j, 1 - k], sib.at[q, j], sib_ss.at[q, j], sib_rs.at[q, j], sibling))

    def backward_single(dist):
        there = chip_at(dist)
        needed = there <= z

        @pl.when(jnp.logical_and(upper, needed))
        def _():
            backward_blocks([(there, 1, dist), (y * NZ + there, 0, dist)])

        @pl.when(upper != needed)
        def _():
            backward_blocks([(there, jnp.where(upper, 1, 0), dist)])

        @pl.when(jnp.logical_not(needed))
        def _():
            no_grads(dist)

        @pl.when(upper)
        def _():
            swap_grads(dist, 1)

        swap_grads(dist, 0)

    def backward_other_row(dist):
        backward_blocks([(chip_at(dist), 1, dist), (chip_at(NZ - dist), 1, NZ - dist)])
        swap_grads(dist, 1)

    def backward_own_row(dist):
        behind, before = dist, NZ - dist
        near, far = z >= dist, z + dist >= NZ

        @pl.when(jnp.logical_and(near, far))
        def _():
            backward_blocks(
                [(y * NZ + chip_at(behind), 0, behind), (y * NZ + chip_at(before), 0, before)])

        @pl.when(near != far)
        def _():
            j = jnp.where(near, before, behind)
            backward_blocks([(y * NZ + chip_at(j), 0, j)])
            no_grads(NZ - j)

        @pl.when(jnp.logical_not(jnp.logical_or(near, far)))
        def _():
            no_grads(before)
            no_grads(behind)

        swap_grads(dist, 0)

    def add_into(ref, parts):
        value = ref[...].astype(F32)
        for part in parts:
            value = value + part[...].astype(F32)
        ref[...] = value.astype(BF)

    def kv_across(dist):
        for side in sides_of(dist):
            j = j_of(side, dist)
            got(sib.at[1, j], sib_rs.at[1, j])
            add_into(dkv.at[1, j, k], [sib.at[1, j]])
            send(upper, lambda j=j: copy(
                dkv.at[1, j, k], yvx.at[j], yv_ss.at[j], yv_rs.at[j], across))

    def kv_pass(dist):
        for side in sides_of(dist):
            j = j_of(side, dist)
            got(sib.at[0, j], sib_rs.at[0, j])
            parts = [sib.at[0, j]]
            for way in ((0, 1) if dist == 0 else (side,) if dist < 3 else ()):
                got(rrx.at[way, dist], rrx_rs.at[way, dist])
                parts.append(rrx.at[way, dist])

            @pl.when(lower)
            def _():
                got(yvx.at[j], yv_rs.at[j])
                add_into(dkv.at[0, j, k], parts + [yvx.at[j]])

            @pl.when(upper)
            def _():
                add_into(dkv.at[0, j, k], parts)

            if dist == 3:
                half = pl.ds(side * 96, 96)
                got(rrx.at[side, 3, half], rrx_rs.at[side, 3])
                add_into(dkv.at[0, j, k, half], [rrx.at[side, 3, half]])
        for side in ((0, 1) if dist > 0 else ()):
            def make(side=side):
                if dist == 4:
                    half = pl.ds(side * 96, 96)
                    src, dst = dkv.at[0, 4, k, half], rrx.at[side, 3, half]
                else:
                    src, dst = dkv.at[0, j_of(side, dist), k], rrx.at[side, dist - 1]
                return copy(src, dst, rrx_ss.at[side, dist - 1],
                            rrx_rs.at[side, dist - 1], ring[side])
            send(None, make)

    def proj_pass(dist):
        for side in sides_of(dist):
            j = j_of(side, dist)
            slot = pj_slot(j, k)
            got(pjs.at[j], pjs_rs.at[j])
            parts = [pjs.at[j]]
            if 0 < dist < 3:
                got(pjr.at[side, dist], pjr_rs.at[side, dist])
                parts.append(pjr.at[side, dist])
            elif dist == 0:
                for other in (0, 1):
                    got(pjr.at[other, 0], pjr_rs.at[other, 0])
                    parts.append(pjr.at[other, 0])
            add_into(pj.at[slot], parts)
            if dist == 3:
                half = pl.ds(side * 64, 64)
                got(pjr.at[side, 3, half], pjr_rs.at[side, 3])
                add_into(pj.at[slot, half], [pjr.at[side, 3, half]])
        if dist == 0:
            return
        for side in (0, 1):
            def make(side=side):
                if dist == 4:
                    half = pl.ds(side * 64, 64)
                    src, dst = pj.at[pj_slot(4, k), half], pjr.at[side, 3, half]
                else:
                    src, dst = pj.at[pj_slot(j_of(side, dist), k)], pjr.at[side, dist - 1]
                return copy(src, dst, pjr_ss.at[side, dist - 1],
                            pjr_rs.at[side, dist - 1], ring[side])
            send(None, make)

    proj_terms()
    proj_pass(4)
    head_grads_done()
    backward_single(4)
    for dist in (3, 2, 1):
        @pl.when(upper)
        def _():
            backward_other_row(dist)
            kv_across(dist + 1)

        kv_pass(dist + 1)
        backward_own_row(dist)
        proj_pass(dist)

    backward_single(0)

    @pl.when(upper)
    def _():
        kv_across(1)

    kv_pass(1)

    query_rows = (dqt[...] * SCALE).T.astype(BF)
    empty = jnp.zeros((TOKENS - SLOTS, HEAD), BF)
    for h in range(HEADS):
        part = jnp.concatenate([query_rows[h * SLOTS:(h + 1) * SLOTS, :], empty], axis=0)
        qo_ref[:, h * HEAD:(h + 1) * HEAD] = mm(pickt[...], part).astype(BF)

    @pl.when(upper)
    def _():
        kv_across(0)

    proj_pass(0)
    po_ref[...] = pj[pj_slot(0, k)]
    kv_pass(0)
    sums = jnp.concatenate(
        [dkv[0, 0, k], jnp.zeros((TOKENS - SLOTS, 2 * HEAD), BF)], axis=0)
    kvo_ref[...] = mm(pickt[...], sums).astype(BF)

    for cond, make in pending:
        if cond is None:
            make().wait_send()
        else:
            @pl.when(cond)
            def _():
                make().wait_send()


def shards(queries, keys_values, upstream, out_proj, keep_index):
    keep = keep_index.reshape(1, SLOTS)
    dma = pltpu.SemaphoreType.DMA
    width = HEADS * HEAD
    vmem = pltpu.VMEM
    scratch = [
        vmem((4 * NZ, ROWS, 2 * HEAD), BF),
        vmem((2 * NZ, 128, width), BF),
        vmem((NX, 2, SLOTS, width), BF),
        vmem((SLOTS, width), BF),
        vmem((2 * NZ, PAIR, QROWS), BF),
        vmem((2 * NZ, 8, QROWS), F32),
        vmem((QROWS, HEAD), BF),
        vmem((QROWS, HEAD), BF),
        vmem((HEAD, QROWS), F32),
        vmem((HEAD, QROWS), F32),
        vmem((8, QROWS), F32),
        vmem((TOKENS, TOKENS), BF),
        vmem((2, SLOTS, width), BF),
        vmem((2, SLOTS, width), F32),
        vmem((SLOTS, width), BF),
        vmem((SLOTS, width), BF),
        vmem((8, TOKENS), jnp.int32),
        vmem((2 * NZ, 128, width), BF),
        vmem((NZ, 128, width), BF),
        vmem((2, 4, 128, width), BF),
        vmem((2, NZ, 2, SLOTS, 2 * HEAD), BF),
        vmem((2, NZ, SLOTS, 2 * HEAD), BF),
        vmem((2, 4, SLOTS, 2 * HEAD), BF),
        vmem((NZ, SLOTS, 2 * HEAD), BF),
        dma((2, 2, 5)), dma((2, 2, 5)), dma((2, 2, 5)), dma((2, 2, 5)),
        dma((2, 5)), dma((2, 5)), dma((2, 5)), dma((2, 5)),
        dma((2, 5)), dma((2, 5)), dma((2, 5)), dma((2, 5)),
        dma((2, 2, 3)), dma((2, 2, 3)), dma((2,)), dma((2,)), dma((2,)),
        dma((NZ,)), dma((NZ,)), dma((2, 4)), dma((2, 4)),
        dma((2, NZ)), dma((2, NZ)), dma((2, 4)), dma((2, 4)),
        dma((NZ,)), dma((NZ,)),
    ]
    return pl.pallas_call(
        kernel,
        out_shape=(
            jax.ShapeDtypeStruct(queries.shape, BF),
            jax.ShapeDtypeStruct(keys_values.shape, BF),
            jax.ShapeDtypeStruct(out_proj.shape, BF),
        ),
        in_specs=[pl.BlockSpec(memory_space=pltpu.VMEM)] * 5,
        out_specs=[pl.BlockSpec(memory_space=pltpu.VMEM)] * 3,
        scratch_shapes=scratch,
        compiler_params=pltpu.CompilerParams(
            collective_id=0, has_side_effects=True, vmem_limit_bytes=56 * 1024 * 1024
        ),
    )(keep, queries, keys_values, upstream, out_proj)


def solution(mesh):
    in_specs = (P("ctx", "tp"), P("ctx", "tp"), P("ctx", "tp"), P("ctx", "tp"), P("ctx"))
    out_specs = (P("ctx", "tp"), P("ctx", "tp"), P("ctx", "tp"))
    return jax.shard_map(shards, mesh=mesh, in_specs=in_specs, out_specs=out_specs, check_vma=False)
```

```python
import functools
import math

import jax
import jax.numpy as jnp
from jax import lax
from jax.experimental import pallas as pl
from jax.experimental.pallas import tpu as pltpu
from jax.sharding import PartitionSpec as P

MESH = pl.DeviceIdType.MESH
BF = jnp.bfloat16
F32 = jnp.float32
NEG = -1e30
HEAD = 128
HEADS = 4
SLOTS = 192
ROWS = SLOTS + 16
PAIR = 2 * SLOTS
QROWS = HEADS * SLOTS
TOKENS = 256
CHUNK = 256
NZ = 8
NX = 4
SCALE = 1.0 / math.sqrt(HEAD)
LOG2 = SCALE * math.log2(math.e)
NT = (((1,), (1,)), ((), ()))


def mm(a, b):
    return jnp.dot(a, b, preferred_element_type=F32)


def kernel(
    keep_ref, q_ref, kv_ref, up_ref, w_ref,
    qo_ref, kvo_ref, po_ref,
    kvb, wb, ub, uown, eb, mb, qr, dor, ot, dqt, stat, pickt, attn, doacc, dsend, drecv, keeps,
    pj, pjs, pjr, dkv, sib, rrx, yvx,
    kv_rs, kv_ss, kvsib_rs, kvsib_ss, vy_rs, vy_ss, vsib_rs, vsib_ss,
    w_rs, w_ss, wsib_rs, wsib_ss,
    u_rs, u_ss, uo_ss, do_s, at_s,
    pjs_rs, pjs_ss, pjr_rs, pjr_ss,
    sib_rs, sib_ss, rrx_rs, rrx_ss, yv_rs, yv_ss,
):
    ctx = lax.axis_index("ctx")
    tp = lax.axis_index("tp")
    y = ctx // (2 * NZ)
    z = (ctx // 2) % NZ
    k = ctx % 2
    yh = tp // NX
    x = tp % NX

    def at_z(zz):
        return y * 2 * NZ + (zz % NZ) * 2 + k

    ring = ((at_z(z + 1), tp), (at_z(z + NZ - 1), tp))
    sibling = (ctx + 1 - 2 * k, tp)
    across = ((1 - y) * 2 * NZ + z * 2 + k, tp)
    xring = ((ctx, yh * NX + (x + 1) % NX), (ctx, yh * NX + (x + NX - 1) % NX))
    yh_peer = (ctx, (1 - yh) * NX + x)
    diagonal = (across[0], yh_peer[1])
    upper = y == 1
    lower = y == 0
    aligned = y == yh
    crossed = y != yh

    barrier = pltpu.get_barrier_semaphore()
    peers = ring + (sibling, across) + xring + (yh_peer, diagonal)
    for peer in peers:
        pl.semaphore_signal(barrier, inc=1, device_id=peer, device_id_type=MESH)

    pending = []

    def copy(src, dst, ssem, rsem, dev):
        return pltpu.make_async_remote_copy(
            src_ref=src, dst_ref=dst, send_sem=ssem, recv_sem=rsem,
            device_id=dev, device_id_type=MESH,
        )

    def send(cond, make):
        pending.append((cond, make))
        make().start()

    def got(ref, sem):
        copy(ref, ref, sem, sem, sibling).wait_recv()

    keeps[0:1, :] = jnp.full((1, TOKENS), -1, jnp.int32)
    keeps[0:1, 0:SLOTS] = keep_ref[...]
    keep = keeps[0:1, :]
    pick_t = jnp.where(
        lax.broadcasted_iota(jnp.int32, (TOKENS, TOKENS), 0) == keep, 1.0, 0.0
    ).astype(F32)
    pickt[...] = pick_t.astype(BF)
    pick = pick_t.T.astype(BF)[:SLOTS]
    count = jnp.sum(jnp.where(keep >= 0, 1.0, 0.0), axis=1, keepdims=True)
    kvb[ctx, 0:SLOTS, :] = mm(pick, kv_ref[...]).astype(BF)
    kvb[ctx, SLOTS:ROWS, :] = jnp.broadcast_to(count, (ROWS - SLOTS, 2 * HEAD)).astype(BF)
    uown[...] = mm(pick, up_ref[...]).astype(BF)
    wb[ctx % (2 * NZ)] = w_ref[...]

    @pl.when(aligned)
    def _():
        ub[x, 0] = uown[...]

    pl.semaphore_wait(barrier, len(peers))

    def slot_of(row, side, dist):
        zz = (z + NZ - dist) % NZ if side == 0 else (z + dist) % NZ
        return row * 2 * NZ + zz * 2 + k

    def kv_part(slot, side, dist, cols):
        if dist < 4:
            rows = pl.ds(0, ROWS)
        else:
            rows = pl.ds(0, 112) if side == 0 else pl.ds(112, 96)
        return kvb.at[slot, rows, cols]

    ALL, KEY, VALUE = pl.ds(0, 2 * HEAD), pl.ds(0, HEAD), pl.ds(HEAD, HEAD)

    def w_part(slot, side, dist):
        if dist < 4:
            return wb.at[slot]
        return wb.at[slot, pl.ds(side * 64, 64)]

    rows_of = (y, 0)
    cols_of = (ALL, KEY)

    def kv_ring(q, side, dist, cond=None):
        part = lambda: kv_part(slot_of(rows_of[q], side, dist), side, dist + 1, cols_of[q])
        send(cond, lambda: copy(
            part(), part(), kv_ss.at[q, side, dist], kv_rs.at[q, side, dist + 1], ring[side]))

    def kv_sib(q, side, dist, cond=None):
        part = lambda: kv_part(slot_of(rows_of[q], side, dist), side, dist, cols_of[q])
        send(cond, lambda: copy(
            part(), part(), kvsib_ss.at[q, side, dist], kvsib_rs.at[q, side, dist], sibling))

    def kv_sib_got(q, side, dist):
        slot = slot_of(rows_of[q], side, dist) + 1 - 2 * k
        got(kv_part(slot, side, dist, cols_of[q]), kvsib_rs.at[q, side, dist])

    def across_cols(dist):
        return VALUE if dist == 1 else ALL

    def v_out(side, dist):
        part = lambda: kv_part(slot_of(0, side, dist), side, dist, across_cols(dist))
        send(lower, lambda: copy(
            part(), part(), vy_ss.at[side, dist], vy_rs.at[side, dist], across))

    def v_across(side, dist):
        part = lambda: kv_part(slot_of(0, side, dist), side, dist, across_cols(dist))
        got(part(), vy_rs.at[side, dist])
        send(upper, lambda: copy(
            part(), part(), vsib_ss.at[side, dist], vsib_rs.at[side, dist], sibling))

    def v_sib_got(side, dist):
        slot = slot_of(0, side, dist) + 1 - 2 * k
        got(kv_part(slot, side, dist, across_cols(dist)), vsib_rs.at[side, dist])

    def w_ring(side, dist):
        part = lambda: w_part(slot_of(0, side, dist), side, dist + 1)
        send(None, lambda: copy(
            part(), part(), w_ss.at[side, dist], w_rs.at[side, dist + 1], ring[side]))

    def w_sib(side, dist):
        part = lambda: w_part(slot_of(0, side, dist), side, dist)
        send(None, lambda: copy(
            part(), part(), wsib_ss.at[side, dist], wsib_rs.at[side, dist], sibling))

    def w_sib_got(side, dist):
        got(w_part(slot_of(0, side, dist) + 1 - 2 * k, side, dist), wsib_rs.at[side, dist])

    def u_part(h, side, dist, half):
        xx = (x + NX - dist) % NX if side == 0 else (x + dist) % NX
        return ub.at[xx, h, pl.ds(side * 96, 96)] if half else ub.at[xx, h]

    def u_ring(h, side, dist, cond=None):
        part = lambda: u_part(h, side, dist, dist + 1 == 2)
        send(cond, lambda: copy(
            part(), part(), u_ss.at[h, side, dist], u_rs.at[h, side, dist + 1], xring[side]))

    def u_got(h, side, dist):
        got(u_part(h, side, dist, dist == 2), u_rs.at[h, side, dist])

    for side in (0, 1):
        kv_ring(0, side, 0)

    @pl.when(aligned)
    def _():
        send(aligned, lambda: copy(uown, ub.at[x, 0], uo_ss.at[0], u_rs.at[0, 0, 0], yh_peer))

    @pl.when(crossed)
    def _():
        send(crossed, lambda: copy(uown, ub.at[x, 1], uo_ss.at[0], u_rs.at[1, 0, 0], across))
        send(crossed, lambda: copy(uown, ub.at[x, 1], uo_ss.at[1], u_rs.at[1, 0, 0], diagonal))

    @pl.when(aligned)
    def _():
        for side in (0, 1):
            u_ring(0, side, 0, aligned)

    kv_sib(0, 0, 0)

    @pl.when(lower)
    def _():
        v_out(0, 0)

    q_kept = mm(pick, q_ref[...]).astype(BF)
    for h in range(HEADS):
        qr[h * SLOTS:(h + 1) * SLOTS, :] = q_kept[:, h * HEAD:(h + 1) * HEAD]

    ot[...] = jnp.zeros_like(ot)
    dqt[...] = jnp.zeros_like(dqt)
    stat[0:1, :] = jnp.full((1, QROWS), NEG, F32)
    stat[1:2, :] = jnp.zeros((1, QROWS), F32)

    def load_pair(p):
        block = kvb[pl.ds(2 * p, 2), 0:SLOTS, :]
        return (block[:, :, 0:HEAD].reshape(PAIR, HEAD), block[:, :, HEAD:].reshape(PAIR, HEAD))

    def turned(block):
        return block.astype(F32).T.astype(BF)

    def key_bias(p):
        counts = kvb[pl.ds(2 * p, 2), SLOTS:ROWS, 0:HEAD].astype(F32)
        place = lax.broadcasted_iota(jnp.int32, (SLOTS, HEAD), 0).astype(F32)
        bias = jnp.concatenate(
            [jnp.where(place < counts[i, 0:1, :], 0.0, NEG) for i in (0, 1)], axis=0)
        return jnp.concatenate([bias] * (CHUNK // HEAD), axis=1)

    def forward_blocks(pairs, own=False):
        loaded = [load_pair(p) for p in pairs]
        biases = [key_bias(p) for p in pairs]
        values_t = jnp.concatenate([turned(values) for _, values in loaded], axis=1)
        values_t = jnp.concatenate(
            [values_t, jnp.ones((16, PAIR * len(pairs)), BF)], axis=0)
        old = stat[0:1, :]
        maxima, halves = [], []
        for first in range(0, QROWS, CHUNK):
            cols = slice(first, first + CHUNK)
            new = old[:, cols]
            scores = []
            for (keys, _), bias in zip(loaded, biases):
                part = lax.dot_general(keys, qr[cols, :], NT, preferred_element_type=F32)
                part = part * LOG2 + bias
                if own:
                    row = lax.broadcasted_iota(jnp.int32, (SLOTS, CHUNK), 0)
                    col = (lax.broadcasted_iota(jnp.int32, (SLOTS, CHUNK), 1) + first) % SLOTS
                    part = part + jnp.concatenate(
                        [jnp.where(row - col <= (k - i) * 1024, 0.0, NEG) for i in (0, 1)], axis=0)
                scores.append(part)
                new = jnp.maximum(new, jnp.max(part, axis=0, keepdims=True))
            weights = [jnp.exp2(part - new).astype(BF) for part in scores]
            for p, part in zip(pairs, weights):
                eb[p, :, cols] = part
                mb[p, 0:1, cols] = new
            halves.append(jnp.concatenate(weights, axis=0))
            maxima.append(new)
        new = jnp.concatenate(maxima, axis=1)
        shrink = jnp.exp2(old - new)
        sums = mm(values_t, jnp.concatenate(halves, axis=1))
        ot[...] = ot[...] * shrink + sums[0:HEAD]
        stat[0:1, :] = new
        stat[1:2, :] = stat[1:2, :] * shrink + sums[HEAD:HEAD + 1]

    kv_sib_got(0, 0, 0)
    forward_blocks([y * NZ + z], True)

    for side in (0, 1):
        w_ring(side, 0)
    w_sib(0, 0)

    def sides_of(dist):
        return (0, 1) if 0 < dist < 4 else (0,)

    def chip_at(j):
        return (z + j) % NZ

    def forward_own_row(dist):
        for side in (0, 1):
            kv_sib_got(0, side, dist)
        before, behind = y * NZ + chip_at(NZ - dist), y * NZ + chip_at(dist)
        near, far = z >= dist, z + dist >= NZ

        @pl.when(jnp.logical_and(near, far))
        def _():
            forward_blocks([before, behind])

        @pl.when(near != far)
        def _():
            forward_blocks([jnp.where(near, before, behind)])

    def forward_other_row(dist):
        @pl.when(upper)
        def _():
            for side in ((0, 1) if dist > 0 else (0,)):
                if dist == 1:
                    kv_sib_got(1, side, dist)
                v_sib_got(side, dist)
            forward_blocks([chip_at(NZ - dist), chip_at(dist)] if dist > 0 else [z])

    def forward_opposite():
        for side in (0, 1):
            kv_sib_got(0, side, 4)
        there = chip_at(4)

        @pl.when(upper)
        def _():
            for side in (0, 1):
                v_sib_got(side, 4)

        @pl.when(jnp.logical_and(upper, z >= 4))
        def _():
            forward_blocks([there, y * NZ + there])

        @pl.when(upper != (z >= 4))
        def _():
            forward_blocks([there])

    def other_row_got(dist):
        @pl.when(upper)
        def _():
            for side in ((0, 1) if dist > 0 else (0,)):
                if dist == 1:
                    got(kv_part(slot_of(0, side, 1), side, 1, KEY), kv_rs.at[1, side, 1])
                    kv_sib(1, side, 1, upper)
                v_across(side, dist)
            if dist == 0:
                for side in (0, 1):
                    kv_ring(1, side, 0, upper)

    def w_got(dist):
        for side in (0, 1):
            got(w_part(slot_of(0, side, dist), side, dist), w_rs.at[side, dist])
            if dist < 4:
                w_ring(side, dist)
            w_sib(side, dist)

    def own_row_got(dist):
        for side in (0, 1):
            got(kv_part(slot_of(y, side, dist), side, dist, ALL), kv_rs.at[0, side, dist])
            if dist < 4:
                kv_ring(0, side, dist)
            kv_sib(0, side, dist)

        @pl.when(lower)
        def _():
            for side in (0, 1):
                v_out(side, dist)

    def u_first_got():
        @pl.when(crossed)
        def _():
            got(ub.at[x, 0], u_rs.at[0, 0, 0])
            for side in (0, 1):
                u_ring(0, side, 0, crossed)

        got(ub.at[x, 1], u_rs.at[1, 0, 0])
        for side in (0, 1):
            u_ring(1, side, 0)

    def u_next_got(h):
        for side in (0, 1):
            u_got(h, side, 1)
            u_ring(h, side, 1)

    own_row_got(1)
    w_got(1)
    other_row_got(0)
    u_first_got()
    forward_own_row(1)
    own_row_got(2)
    forward_other_row(0)
    w_got(2)
    other_row_got(1)
    u_next_got(0)
    forward_own_row(2)
    own_row_got(3)
    forward_other_row(1)
    w_got(3)
    other_row_got(2)
    u_next_got(1)
    own_row_got(4)
    forward_own_row(3)
    forward_other_row(2)
    w_got(4)
    other_row_got(3)
    other_row_got(4)
    forward_other_row(3)
    forward_opposite()

    total = stat[1:2, :]
    inv = 1.0 / total
    stat[1:2, :] = inv
    attn_t = (ot[...] * inv).astype(BF).astype(F32)
    ot[...] = attn_t
    attn_rows = attn_t.T.astype(BF)
    for h in range(HEADS):
        attn[0, :, h * HEAD:(h + 1) * HEAD] = attn_rows[h * SLOTS:(h + 1) * SLOTS, :]
    send(None, lambda: copy(attn.at[0], attn.at[1], at_s.at[0], at_s.at[1], across))

    for h in (0, 1):
        for side in (0, 1):
            u_got(h, side, 2)
    for dist in range(0, 5):
        for side in ((0, 1) if dist > 0 else (0,)):
            w_sib_got(side, dist)

    def head_grads(h):
        doacc[h] = jnp.zeros((SLOTS, HEADS * HEAD), F32)

        def step(i, carry):
            doacc[h] += mm(ub[i, h], wb[pl.ds(4 * i, 4)].reshape(4 * 128, HEADS * HEAD))
            return carry

        lax.fori_loop(0, NX, step, 0)

    head_grads(1)
    dsend[...] = doacc[1].astype(BF)
    send(None, lambda: copy(dsend, drecv, do_s.at[0], do_s.at[1], across))
    head_grads(0)

    def pj_slot(j, core):
        return ((z + j) % NZ) * 2 + core

    def proj_swap(j):
        return copy(pj.at[pj_slot(j, 1 - k)], pjs.at[j], pjs_ss.at[j], pjs_rs.at[j], sibling)

    def proj_terms(first, last):
        def step(i, carry):
            xx = (((z + NZ // 2) % NZ) // 2 + jnp.where(i < 2, i, 5 - i)) % NX
            block = ub[xx].reshape(PAIR, HEADS * HEAD).astype(F32)
            term = mm(block.T.astype(BF), attn[...].reshape(PAIR, HEADS * HEAD)).astype(BF)
            pj[pl.ds(4 * xx, 4)] = term.reshape(4, 128, HEADS * HEAD)
            for i in (0, 1):
                proj_swap((2 * xx + i + NZ - z) % NZ).start()
            return carry

        lax.fori_loop(first, last, step, 0)

    def head_grads_done():
        got(drecv, do_s.at[1])
        for h in range(HEADS):
            cols = slice(h * HEAD, (h + 1) * HEAD)
            grads = (doacc[0, :, cols] + drecv[:, cols].astype(F32)).astype(BF)
            dor[h * SLOTS:(h + 1) * SLOTS, :] = grads
        stat[2:3, :] = jnp.sum(dor[...].astype(F32).T * ot[...], axis=0, keepdims=True)

    def backward_blocks(items):
        loaded = [load_pair(p) for p, _, _ in items]
        keys_t = jnp.concatenate([turned(keys) for keys, _ in loaded], axis=1)
        values = jnp.concatenate([values for _, values in loaded], axis=0)
        probs = jnp.concatenate([
            eb[p].astype(F32) * (jnp.exp2(mb[p, 0:1, :] - stat[0:1, :]) * stat[1:2, :])
            for p, _, _ in items], axis=0)
        grads = dor[...]
        value_grad = mm(probs.astype(BF), grads)
        pushes = lax.dot_general(values, grads, NT, preferred_element_type=F32)
        slopes = (probs * (pushes - stat[2:3, :])).astype(BF)
        key_grad = mm(slopes, qr[...])
        dqt[...] += mm(keys_t, slopes)
        for i, (_, q, j) in enumerate(items):
            rows = slice(i * PAIR, (i + 1) * PAIR)
            dkv[q, j, :, :, 0:HEAD] = (key_grad[rows] * SCALE).astype(BF).reshape(2, SLOTS, HEAD)
            dkv[q, j, :, :, HEAD:] = value_grad[rows].astype(BF).reshape(2, SLOTS, HEAD)

    def no_grads(j):
        dkv[0, j] = jnp.zeros((2, SLOTS, 2 * HEAD), BF)

    def j_of(side, dist):
        return dist if side == 0 else NZ - dist

    def swap_grads(dist, q):
        for side in sides_of(dist):
            j = j_of(side, dist)
            send(upper if q else None, lambda j=j: copy(
                dkv.at[q, j, 1 - k], sib.at[q, j], sib_ss.at[q, j], sib_rs.at[q, j], sibling))

    def backward_single(dist):
        there = chip_at(dist)
        needed = there <= z

        @pl.when(jnp.logical_and(upper, needed))
        def _():
            backward_blocks([(there, 1, dist), (y * NZ + there, 0, dist)])

        @pl.when(upper != needed)
        def _():
            backward_blocks([(there, jnp.where(upper, 1, 0), dist)])

        @pl.when(jnp.logical_not(needed))
        def _():
            no_grads(dist)

        @pl.when(upper)
        def _():
            swap_grads(dist, 1)

        swap_grads(dist, 0)

    def backward_other_row(dist):
        backward_blocks([(chip_at(dist), 1, dist), (chip_at(NZ - dist), 1, NZ - dist)])
        swap_grads(dist, 1)

    def backward_own_row(dist):
        behind, before = dist, NZ - dist
        near, far = z >= dist, z + dist >= NZ

        @pl.when(jnp.logical_and(near, far))
        def _():
            backward_blocks(
                [(y * NZ + chip_at(behind), 0, behind), (y * NZ + chip_at(before), 0, before)])

        @pl.when(near != far)
        def _():
            j = jnp.where(near, before, behind)
            backward_blocks([(y * NZ + chip_at(j), 0, j)])
            no_grads(NZ - j)

        @pl.when(jnp.logical_not(jnp.logical_or(near, far)))
        def _():
            no_grads(before)
            no_grads(behind)

        swap_grads(dist, 0)

    def add_into(ref, parts):
        value = ref[...].astype(F32)
        for part in parts:
            value = value + part[...].astype(F32)
        ref[...] = value.astype(BF)

    def kv_across(dist):
        for side in sides_of(dist):
            j = j_of(side, dist)
            got(sib.at[1, j], sib_rs.at[1, j])
            add_into(dkv.at[1, j, k], [sib.at[1, j]])
            send(upper, lambda j=j: copy(
                dkv.at[1, j, k], yvx.at[j], yv_ss.at[j], yv_rs.at[j], across))

    def kv_pass(dist):
        for side in sides_of(dist):
            j = j_of(side, dist)
            got(sib.at[0, j], sib_rs.at[0, j])
            parts = [sib.at[0, j]]
            for way in ((0, 1) if dist == 0 else (side,) if dist < 3 else ()):
                got(rrx.at[way, dist], rrx_rs.at[way, dist])
                parts.append(rrx.at[way, dist])

            @pl.when(lower)
            def _():
                got(yvx.at[j], yv_rs.at[j])
                add_into(dkv.at[0, j, k], parts + [yvx.at[j]])

            @pl.when(upper)
            def _():
                add_into(dkv.at[0, j, k], parts)

            if dist == 3:
                half = pl.ds(side * 96, 96)
                got(rrx.at[side, 3, half], rrx_rs.at[side, 3])
                add_into(dkv.at[0, j, k, half], [rrx.at[side, 3, half]])
        for side in ((0, 1) if dist > 0 else ()):
            def make(side=side):
                if dist == 4:
                    half = pl.ds(side * 96, 96)
                    src, dst = dkv.at[0, 4, k, half], rrx.at[side, 3, half]
                else:
                    src, dst = dkv.at[0, j_of(side, dist), k], rrx.at[side, dist - 1]
                return copy(src, dst, rrx_ss.at[side, dist - 1],
                            rrx_rs.at[side, dist - 1], ring[side])
            send(None, make)

    def proj_pass(dist):
        for side in sides_of(dist):
            j = j_of(side, dist)
            slot = pj_slot(j, k)
            got(pjs.at[j], pjs_rs.at[j])
            parts = [pjs.at[j]]
            if 0 < dist < 3:
                got(pjr.at[side, dist], pjr_rs.at[side, dist])
                parts.append(pjr.at[side, dist])
            elif dist == 0:
                for other in (0, 1):
                    got(pjr.at[other, 0], pjr_rs.at[other, 0])
                    parts.append(pjr.at[other, 0])
            add_into(pj.at[slot], parts)
            if dist == 3:
                half = pl.ds(side * 64, 64)
                got(pjr.at[side, 3, half], pjr_rs.at[side, 3])
                add_into(pj.at[slot, half], [pjr.at[side, 3, half]])
        if dist == 0:
            return
        for side in (0, 1):
            def make(side=side):
                if dist == 4:
                    half = pl.ds(side * 64, 64)
                    src, dst = pj.at[pj_slot(4, k), half], pjr.at[side, 3, half]
                else:
                    src, dst = pj.at[pj_slot(j_of(side, dist), k)], pjr.at[side, dist - 1]
                return copy(src, dst, pjr_ss.at[side, dist - 1],
                            pjr_rs.at[side, dist - 1], ring[side])
            send(None, make)

    got(attn.at[1], at_s.at[1])
    proj_terms(0, 2)
    proj_pass(4)
    proj_terms(2, NX)
    for j in range(NZ):
        pending.append((None, lambda j=j: proj_swap(j)))
    head_grads_done()
    backward_single(4)
    for dist in (3, 2, 1):
        @pl.when(upper)
        def _():
            backward_other_row(dist)
            kv_across(dist + 1)

        kv_pass(dist + 1)
        backward_own_row(dist)
        proj_pass(dist)

    backward_single(0)

    @pl.when(upper)
    def _():
        kv_across(1)

    kv_pass(1)

    query_rows = (dqt[...] * SCALE).T.astype(BF)
    empty = jnp.zeros((TOKENS - SLOTS, HEAD), BF)
    for h in range(HEADS):
        part = jnp.concatenate([query_rows[h * SLOTS:(h + 1) * SLOTS, :], empty], axis=0)
        qo_ref[:, h * HEAD:(h + 1) * HEAD] = mm(pickt[...], part).astype(BF)

    @pl.when(upper)
    def _():
        kv_across(0)

    proj_pass(0)
    po_ref[...] = pj[pj_slot(0, k)]
    kv_pass(0)
    sums = jnp.concatenate(
        [dkv[0, 0, k], jnp.zeros((TOKENS - SLOTS, 2 * HEAD), BF)], axis=0)
    kvo_ref[...] = mm(pickt[...], sums).astype(BF)

    for cond, make in pending:
        if cond is None:
            make().wait_send()
        else:
            @pl.when(cond)
            def _():
                make().wait_send()


def shards(queries, keys_values, upstream, out_proj, keep_index):
    keep = keep_index.reshape(1, SLOTS)
    dma = pltpu.SemaphoreType.DMA
    width = HEADS * HEAD
    vmem = pltpu.VMEM
    scratch = [
        vmem((4 * NZ, ROWS, 2 * HEAD), BF),
        vmem((2 * NZ, 128, width), BF),
        vmem((NX, 2, SLOTS, width), BF),
        vmem((SLOTS, width), BF),
        vmem((2 * NZ, PAIR, QROWS), BF),
        vmem((2 * NZ, 8, QROWS), F32),
        vmem((QROWS, HEAD), BF),
        vmem((QROWS, HEAD), BF),
        vmem((HEAD, QROWS), F32),
        vmem((HEAD, QROWS), F32),
        vmem((8, QROWS), F32),
        vmem((TOKENS, TOKENS), BF),
        vmem((2, SLOTS, width), BF),
        vmem((2, SLOTS, width), F32),
        vmem((SLOTS, width), BF),
        vmem((SLOTS, width), BF),
        vmem((8, TOKENS), jnp.int32),
        vmem((2 * NZ, 128, width), BF),
        vmem((NZ, 128, width), BF),
        vmem((2, 4, 128, width), BF),
        vmem((2, NZ, 2, SLOTS, 2 * HEAD), BF),
        vmem((2, NZ, SLOTS, 2 * HEAD), BF),
        vmem((2, 4, SLOTS, 2 * HEAD), BF),
        vmem((NZ, SLOTS, 2 * HEAD), BF),
        dma((2, 2, 5)), dma((2, 2, 5)), dma((2, 2, 5)), dma((2, 2, 5)),
        dma((2, 5)), dma((2, 5)), dma((2, 5)), dma((2, 5)),
        dma((2, 5)), dma((2, 5)), dma((2, 5)), dma((2, 5)),
        dma((2, 2, 3)), dma((2, 2, 3)), dma((2,)), dma((2,)), dma((2,)),
        dma((NZ,)), dma((NZ,)), dma((2, 4)), dma((2, 4)),
        dma((2, NZ)), dma((2, NZ)), dma((2, 4)), dma((2, 4)),
        dma((NZ,)), dma((NZ,)),
    ]
    return pl.pallas_call(
        kernel,
        out_shape=(
            jax.ShapeDtypeStruct(queries.shape, BF),
            jax.ShapeDtypeStruct(keys_values.shape, BF),
            jax.ShapeDtypeStruct(out_proj.shape, BF),
        ),
        in_specs=[pl.BlockSpec(memory_space=pltpu.VMEM)] * 5,
        out_specs=[pl.BlockSpec(memory_space=pltpu.VMEM)] * 3,
        scratch_shapes=scratch,
        compiler_params=pltpu.CompilerParams(
            collective_id=0, has_side_effects=True, vmem_limit_bytes=56 * 1024 * 1024
        ),
    )(keep, queries, keys_values, upstream, out_proj)


def solution(mesh):
    in_specs = (P("ctx", "tp"), P("ctx", "tp"), P("ctx", "tp"), P("ctx", "tp"), P("ctx"))
    out_specs = (P("ctx", "tp"), P("ctx", "tp"), P("ctx", "tp"))
    return jax.shard_map(shards, mesh=mesh, in_specs=in_specs, out_specs=out_specs, check_vma=False)
```

```python
import functools
import math

import jax
import jax.numpy as jnp
from jax import lax
from jax.experimental import pallas as pl
from jax.experimental.pallas import tpu as pltpu
from jax.sharding import PartitionSpec as P

MESH = pl.DeviceIdType.MESH
BF = jnp.bfloat16
F32 = jnp.float32
NEG = -1e30
HEAD = 128
HEADS = 4
SLOTS = 192
ROWS = SLOTS + 16
PAIR = 2 * SLOTS
QROWS = HEADS * SLOTS
TOKENS = 256
CHUNK = 256
NZ = 8
NX = 4
SCALE = 1.0 / math.sqrt(HEAD)
LOG2 = SCALE * math.log2(math.e)
NT = (((1,), (1,)), ((), ()))


def mm(a, b):
    return jnp.dot(a, b, preferred_element_type=F32)


def kernel(
    keep_ref, q_ref, kv_ref, up_ref, w_ref,
    qo_ref, kvo_ref, po_ref,
    kvb, wb, ub, uown, eb, mb, qr, dor, ot, dqt, stat, pickt, attn, doacc, dsend, drecv, keeps,
    pj, pjs, pjr, dkv, sib, rrx, yvx,
    kv_rs, kv_ss, kvsib_rs, kvsib_ss, vy_rs, vy_ss, vsib_rs, vsib_ss,
    w_rs, w_ss, wsib_rs, wsib_ss,
    u_rs, u_ss, uo_ss, do_s, at_s,
    pjs_rs, pjs_ss, pjr_rs, pjr_ss,
    sib_rs, sib_ss, rrx_rs, rrx_ss, yv_rs, yv_ss,
):
    ctx = lax.axis_index("ctx")
    tp = lax.axis_index("tp")
    y = ctx // (2 * NZ)
    z = (ctx // 2) % NZ
    k = ctx % 2
    yh = tp // NX
    x = tp % NX

    def at_z(zz):
        return y * 2 * NZ + (zz % NZ) * 2 + k

    ring = ((at_z(z + 1), tp), (at_z(z + NZ - 1), tp))
    sibling = (ctx + 1 - 2 * k, tp)
    across = ((1 - y) * 2 * NZ + z * 2 + k, tp)
    xring = ((ctx, yh * NX + (x + 1) % NX), (ctx, yh * NX + (x + NX - 1) % NX))
    yh_peer = (ctx, (1 - yh) * NX + x)
    diagonal = (across[0], yh_peer[1])
    upper = y == 1
    lower = y == 0
    aligned = y == yh
    crossed = y != yh

    barrier = pltpu.get_barrier_semaphore()
    peers = ring + (sibling, across) + xring + (yh_peer, diagonal)
    for peer in peers:
        pl.semaphore_signal(barrier, inc=1, device_id=peer, device_id_type=MESH)

    pending = []

    def copy(src, dst, ssem, rsem, dev):
        return pltpu.make_async_remote_copy(
            src_ref=src, dst_ref=dst, send_sem=ssem, recv_sem=rsem,
            device_id=dev, device_id_type=MESH,
        )

    def send(cond, make):
        pending.append((cond, make))
        make().start()

    def got(ref, sem):
        copy(ref, ref, sem, sem, sibling).wait_recv()

    keeps[0:1, :] = jnp.full((1, TOKENS), -1, jnp.int32)
    keeps[0:1, 0:SLOTS] = keep_ref[...]
    keep = keeps[0:1, :]
    pick_t = jnp.where(
        lax.broadcasted_iota(jnp.int32, (TOKENS, TOKENS), 0) == keep, 1.0, 0.0
    ).astype(F32)
    pickt[...] = pick_t.astype(BF)
    pick = pick_t.T.astype(BF)[:SLOTS]
    count = jnp.sum(jnp.where(keep >= 0, 1.0, 0.0), axis=1, keepdims=True)
    kvb[ctx, 0:SLOTS, :] = mm(pick, kv_ref[...]).astype(BF)
    kvb[ctx, SLOTS:ROWS, :] = jnp.broadcast_to(count, (ROWS - SLOTS, 2 * HEAD)).astype(BF)
    uown[...] = mm(pick, up_ref[...]).astype(BF)
    wb[ctx % (2 * NZ)] = w_ref[...]

    @pl.when(aligned)
    def _():
        ub[x, 0] = uown[...]

    pl.semaphore_wait(barrier, len(peers))

    def slot_of(row, side, dist):
        zz = (z + NZ - dist) % NZ if side == 0 else (z + dist) % NZ
        return row * 2 * NZ + zz * 2 + k

    def kv_part(slot, side, dist, cols):
        if dist < 4:
            rows = pl.ds(0, ROWS)
        else:
            rows = pl.ds(0, 112) if side == 0 else pl.ds(112, 96)
        return kvb.at[slot, rows, cols]

    ALL, KEY, VALUE = pl.ds(0, 2 * HEAD), pl.ds(0, HEAD), pl.ds(HEAD, HEAD)

    def w_part(slot, side, dist):
        if dist < 4:
            return wb.at[slot]
        return wb.at[slot, pl.ds(side * 64, 64)]

    rows_of = (y, 0)
    cols_of = (ALL, KEY)

    def kv_ring(q, side, dist, cond=None):
        part = lambda: kv_part(slot_of(rows_of[q], side, dist), side, dist + 1, cols_of[q])
        send(cond, lambda: copy(
            part(), part(), kv_ss.at[q, side, dist], kv_rs.at[q, side, dist + 1], ring[side]))

    def kv_sib(q, side, dist, cond=None):
        part = lambda: kv_part(slot_of(rows_of[q], side, dist), side, dist, cols_of[q])
        send(cond, lambda: copy(
            part(), part(), kvsib_ss.at[q, side, dist], kvsib_rs.at[q, side, dist], sibling))

    def kv_sib_got(q, side, dist):
        slot = slot_of(rows_of[q], side, dist) + 1 - 2 * k
        got(kv_part(slot, side, dist, cols_of[q]), kvsib_rs.at[q, side, dist])

    def across_cols(dist):
        return VALUE if dist == 1 else ALL

    def v_out(side, dist):
        part = lambda: kv_part(slot_of(0, side, dist), side, dist, across_cols(dist))
        send(lower, lambda: copy(
            part(), part(), vy_ss.at[side, dist], vy_rs.at[side, dist], across))

    def v_across(side, dist):
        part = lambda: kv_part(slot_of(0, side, dist), side, dist, across_cols(dist))
        got(part(), vy_rs.at[side, dist])
        send(upper, lambda: copy(
            part(), part(), vsib_ss.at[side, dist], vsib_rs.at[side, dist], sibling))

    def v_sib_got(side, dist):
        slot = slot_of(0, side, dist) + 1 - 2 * k
        got(kv_part(slot, side, dist, across_cols(dist)), vsib_rs.at[side, dist])

    def w_ring(side, dist):
        part = lambda: w_part(slot_of(0, side, dist), side, dist + 1)
        send(None, lambda: copy(
            part(), part(), w_ss.at[side, dist], w_rs.at[side, dist + 1], ring[side]))

    def w_sib(side, dist):
        part = lambda: w_part(slot_of(0, side, dist), side, dist)
        send(None, lambda: copy(
            part(), part(), wsib_ss.at[side, dist], wsib_rs.at[side, dist], sibling))

    def w_sib_got(side, dist):
        got(w_part(slot_of(0, side, dist) + 1 - 2 * k, side, dist), wsib_rs.at[side, dist])

    def u_part(h, side, dist, half):
        xx = (x + NX - dist) % NX if side == 0 else (x + dist) % NX
        return ub.at[xx, h, pl.ds(side * 96, 96)] if half else ub.at[xx, h]

    def u_ring(h, side, dist, cond=None):
        part = lambda: u_part(h, side, dist, dist + 1 == 2)
        send(cond, lambda: copy(
            part(), part(), u_ss.at[h, side, dist], u_rs.at[h, side, dist + 1], xring[side]))

    def u_got(h, side, dist):
        got(u_part(h, side, dist, dist == 2), u_rs.at[h, side, dist])

    kv_sib(0, 0, 0)
    for side in (0, 1):
        kv_ring(0, side, 0)

    @pl.when(aligned)
    def _():
        send(aligned, lambda: copy(uown, ub.at[x, 0], uo_ss.at[0], u_rs.at[0, 0, 0], yh_peer))

    @pl.when(crossed)
    def _():
        send(crossed, lambda: copy(uown, ub.at[x, 1], uo_ss.at[0], u_rs.at[1, 0, 0], across))
        send(crossed, lambda: copy(uown, ub.at[x, 1], uo_ss.at[1], u_rs.at[1, 0, 0], diagonal))

    @pl.when(aligned)
    def _():
        for side in (0, 1):
            u_ring(0, side, 0, aligned)

    @pl.when(lower)
    def _():
        v_out(0, 0)

    q_kept = mm(pick, q_ref[...]).astype(BF)
    for h in range(HEADS):
        qr[h * SLOTS:(h + 1) * SLOTS, :] = q_kept[:, h * HEAD:(h + 1) * HEAD]

    ot[...] = jnp.zeros_like(ot)
    dqt[...] = jnp.zeros_like(dqt)
    stat[0:1, :] = jnp.full((1, QROWS), NEG, F32)
    stat[1:2, :] = jnp.zeros((1, QROWS), F32)

    def load_pair(p):
        block = kvb[pl.ds(2 * p, 2), 0:SLOTS, :]
        return (block[:, :, 0:HEAD].reshape(PAIR, HEAD), block[:, :, HEAD:].reshape(PAIR, HEAD))

    def turned(block):
        return block.astype(F32).T.astype(BF)

    def key_bias(p):
        counts = kvb[pl.ds(2 * p, 2), SLOTS:ROWS, 0:HEAD].astype(F32)
        place = lax.broadcasted_iota(jnp.int32, (SLOTS, HEAD), 0).astype(F32)
        bias = jnp.concatenate(
            [jnp.where(place < counts[i, 0:1, :], 0.0, NEG) for i in (0, 1)], axis=0)
        return jnp.concatenate([bias] * (CHUNK // HEAD), axis=1)

    def forward_blocks(pairs, own=False):
        loaded = [load_pair(p) for p in pairs]
        biases = [key_bias(p) for p in pairs]
        values_t = jnp.concatenate([turned(values) for _, values in loaded], axis=1)
        values_t = jnp.concatenate(
            [values_t, jnp.ones((16, PAIR * len(pairs)), BF)], axis=0)
        old = stat[0:1, :]
        maxima, halves = [], []
        for first in range(0, QROWS, CHUNK):
            cols = slice(first, first + CHUNK)
            new = old[:, cols]
            scores = []
            for (keys, _), bias in zip(loaded, biases):
                part = lax.dot_general(keys, qr[cols, :], NT, preferred_element_type=F32)
                part = part * LOG2 + bias
                if own:
                    row = lax.broadcasted_iota(jnp.int32, (SLOTS, CHUNK), 0)
                    col = (lax.broadcasted_iota(jnp.int32, (SLOTS, CHUNK), 1) + first) % SLOTS
                    part = part + jnp.concatenate(
                        [jnp.where(row - col <= (k - i) * 1024, 0.0, NEG) for i in (0, 1)], axis=0)
                scores.append(part)
                new = jnp.maximum(new, jnp.max(part, axis=0, keepdims=True))
            weights = [jnp.exp2(part - new).astype(BF) for part in scores]
            for p, part in zip(pairs, weights):
                eb[p, :, cols] = part
                mb[p, 0:1, cols] = new
            halves.append(jnp.concatenate(weights, axis=0))
            maxima.append(new)
        new = jnp.concatenate(maxima, axis=1)
        shrink = jnp.exp2(old - new)
        sums = mm(values_t, jnp.concatenate(halves, axis=1))
        ot[...] = ot[...] * shrink + sums[0:HEAD]
        stat[0:1, :] = new
        stat[1:2, :] = stat[1:2, :] * shrink + sums[HEAD:HEAD + 1]

    for side in (0, 1):
        w_ring(side, 0)
    w_sib(0, 0)

    kv_sib_got(0, 0, 0)
    forward_blocks([y * NZ + z], True)


    def sides_of(dist):
        return (0, 1) if 0 < dist < 4 else (0,)

    def chip_at(j):
        return (z + j) % NZ

    def forward_own_row(dist):
        for side in (0, 1):
            kv_sib_got(0, side, dist)
        before, behind = y * NZ + chip_at(NZ - dist), y * NZ + chip_at(dist)
        near, far = z >= dist, z + dist >= NZ

        @pl.when(jnp.logical_and(near, far))
        def _():
            forward_blocks([before, behind])

        @pl.when(near != far)
        def _():
            forward_blocks([jnp.where(near, before, behind)])

    def forward_other_row(dist):
        @pl.when(upper)
        def _():
            for side in ((0, 1) if dist > 0 else (0,)):
                if dist == 1:
                    kv_sib_got(1, side, dist)
                v_sib_got(side, dist)
            forward_blocks([chip_at(NZ - dist), chip_at(dist)] if dist > 0 else [z])

    def forward_opposite():
        for side in (0, 1):
            kv_sib_got(0, side, 4)
        there = chip_at(4)

        @pl.when(upper)
        def _():
            for side in (0, 1):
                v_sib_got(side, 4)

        @pl.when(jnp.logical_and(upper, z >= 4))
        def _():
            forward_blocks([there, y * NZ + there])

        @pl.when(upper != (z >= 4))
        def _():
            forward_blocks([there])

    def other_row_got(dist):
        @pl.when(upper)
        def _():
            for side in ((0, 1) if dist > 0 else (0,)):
                if dist == 1:
                    got(kv_part(slot_of(0, side, 1), side, 1, KEY), kv_rs.at[1, side, 1])
                    kv_sib(1, side, 1, upper)
                v_across(side, dist)
            if dist == 0:
                for side in (0, 1):
                    kv_ring(1, side, 0, upper)

    def w_got(dist):
        for side in (0, 1):
            got(w_part(slot_of(0, side, dist), side, dist), w_rs.at[side, dist])
            if dist < 4:
                w_ring(side, dist)
            w_sib(side, dist)

    def own_row_got(dist):
        for side in (0, 1):
            got(kv_part(slot_of(y, side, dist), side, dist, ALL), kv_rs.at[0, side, dist])
            if dist < 4:
                kv_ring(0, side, dist)
            kv_sib(0, side, dist)

        @pl.when(lower)
        def _():
            for side in (0, 1):
                v_out(side, dist)

    def u_first_got():
        @pl.when(crossed)
        def _():
            got(ub.at[x, 0], u_rs.at[0, 0, 0])
            for side in (0, 1):
                u_ring(0, side, 0, crossed)

        got(ub.at[x, 1], u_rs.at[1, 0, 0])
        for side in (0, 1):
            u_ring(1, side, 0)

    def u_next_got(h):
        for side in (0, 1):
            u_got(h, side, 1)
            u_ring(h, side, 1)

    own_row_got(1)
    w_got(1)
    other_row_got(0)
    u_first_got()
    forward_own_row(1)
    own_row_got(2)
    forward_other_row(0)
    w_got(2)
    other_row_got(1)
    u_next_got(0)
    forward_own_row(2)
    own_row_got(3)
    forward_other_row(1)
    w_got(3)
    other_row_got(2)
    u_next_got(1)
    own_row_got(4)
    forward_own_row(3)
    forward_other_row(2)
    w_got(4)
    other_row_got(3)
    other_row_got(4)
    forward_other_row(3)
    forward_opposite()

    total = stat[1:2, :]
    inv = 1.0 / total
    stat[1:2, :] = inv
    attn_t = (ot[...] * inv).astype(BF).astype(F32)
    ot[...] = attn_t
    attn_rows = attn_t.T.astype(BF)
    for h in range(HEADS):
        attn[0, :, h * HEAD:(h + 1) * HEAD] = attn_rows[h * SLOTS:(h + 1) * SLOTS, :]
    send(None, lambda: copy(attn.at[0], attn.at[1], at_s.at[0], at_s.at[1], across))

    for h in (0, 1):
        for side in (0, 1):
            u_got(h, side, 2)
    for dist in range(0, 5):
        for side in ((0, 1) if dist > 0 else (0,)):
            w_sib_got(side, dist)

    def head_grads(h):
        doacc[h] = jnp.zeros((SLOTS, HEADS * HEAD), F32)

        def step(i, carry):
            doacc[h] += mm(ub[i, h], wb[pl.ds(4 * i, 4)].reshape(4 * 128, HEADS * HEAD))
            return carry

        lax.fori_loop(0, NX, step, 0)

    head_grads(1)
    dsend[...] = doacc[1].astype(BF)
    send(None, lambda: copy(dsend, drecv, do_s.at[0], do_s.at[1], across))
    head_grads(0)

    def pj_slot(j, core):
        return ((z + j) % NZ) * 2 + core

    def proj_swap(j):
        return copy(pj.at[pj_slot(j, 1 - k)], pjs.at[j], pjs_ss.at[j], pjs_rs.at[j], sibling)

    def proj_terms(first, last):
        def step(i, carry):
            xx = (((z + NZ // 2) % NZ) // 2 + jnp.where(i < 2, i, 5 - i)) % NX
            block = ub[xx].reshape(PAIR, HEADS * HEAD).astype(F32)
            term = mm(block.T.astype(BF), attn[...].reshape(PAIR, HEADS * HEAD)).astype(BF)
            pj[pl.ds(4 * xx, 4)] = term.reshape(4, 128, HEADS * HEAD)
            for i in (0, 1):
                proj_swap((2 * xx + i + NZ - z) % NZ).start()
            return carry

        lax.fori_loop(first, last, step, 0)

    def head_grads_done():
        got(drecv, do_s.at[1])
        for h in range(HEADS):
            cols = slice(h * HEAD, (h + 1) * HEAD)
            grads = (doacc[0, :, cols] + drecv[:, cols].astype(F32)).astype(BF)
            dor[h * SLOTS:(h + 1) * SLOTS, :] = grads
        stat[2:3, :] = jnp.sum(dor[...].astype(F32).T * ot[...], axis=0, keepdims=True)

    def backward_blocks(items):
        loaded = [load_pair(p) for p, _, _ in items]
        keys_t = jnp.concatenate([turned(keys) for keys, _ in loaded], axis=1)
        values = jnp.concatenate([values for _, values in loaded], axis=0)
        probs = jnp.concatenate([
            eb[p].astype(F32) * (jnp.exp2(mb[p, 0:1, :] - stat[0:1, :]) * stat[1:2, :])
            for p, _, _ in items], axis=0)
        grads = dor[...]
        value_grad = mm(probs.astype(BF), grads)
        pushes = lax.dot_general(values, grads, NT, preferred_element_type=F32)
        slopes = (probs * (pushes - stat[2:3, :])).astype(BF)
        key_grad = mm(slopes, qr[...])
        dqt[...] += mm(keys_t, slopes)
        for i, (_, q, j) in enumerate(items):
            rows = slice(i * PAIR, (i + 1) * PAIR)
            dkv[q, j, :, :, 0:HEAD] = (key_grad[rows] * SCALE).astype(BF).reshape(2, SLOTS, HEAD)
            dkv[q, j, :, :, HEAD:] = value_grad[rows].astype(BF).reshape(2, SLOTS, HEAD)

    def no_grads(j):
        dkv[0, j] = jnp.zeros((2, SLOTS, 2 * HEAD), BF)

    def j_of(side, dist):
        return dist if side == 0 else NZ - dist

    def swap_grads(dist, q):
        for side in sides_of(dist):
            j = j_of(side, dist)
            send(upper if q else None, lambda j=j: copy(
                dkv.at[q, j, 1 - k], sib.at[q, j], sib_ss.at[q, j], sib_rs.at[q, j], sibling))

    def backward_single(dist):
        there = chip_at(dist)
        needed = there <= z

        @pl.when(jnp.logical_and(upper, needed))
        def _():
            backward_blocks([(there, 1, dist), (y * NZ + there, 0, dist)])

        @pl.when(upper != needed)
        def _():
            backward_blocks([(there, jnp.where(upper, 1, 0), dist)])

        @pl.when(jnp.logical_not(needed))
        def _():
            no_grads(dist)

        @pl.when(upper)
        def _():
            swap_grads(dist, 1)

        swap_grads(dist, 0)

    def backward_other_row(dist):
        backward_blocks([(chip_at(dist), 1, dist), (chip_at(NZ - dist), 1, NZ - dist)])
        swap_grads(dist, 1)

    def backward_own_row(dist):
        behind, before = dist, NZ - dist
        near, far = z >= dist, z + dist >= NZ

        @pl.when(jnp.logical_and(near, far))
        def _():
            backward_blocks(
                [(y * NZ + chip_at(behind), 0, behind), (y * NZ + chip_at(before), 0, before)])

        @pl.when(near != far)
        def _():
            j = jnp.where(near, before, behind)
            backward_blocks([(y * NZ + chip_at(j), 0, j)])
            no_grads(NZ - j)

        @pl.when(jnp.logical_not(jnp.logical_or(near, far)))
        def _():
            no_grads(before)
            no_grads(behind)

        swap_grads(dist, 0)

    def add_into(ref, parts):
        value = ref[...].astype(F32)
        for part in parts:
            value = value + part[...].astype(F32)
        ref[...] = value.astype(BF)

    def kv_across(dist):
        for side in sides_of(dist):
            j = j_of(side, dist)
            got(sib.at[1, j], sib_rs.at[1, j])
            add_into(dkv.at[1, j, k], [sib.at[1, j]])
            send(upper, lambda j=j: copy(
                dkv.at[1, j, k], yvx.at[j], yv_ss.at[j], yv_rs.at[j], across))

    def kv_pass(dist):
        for side in sides_of(dist):
            j = j_of(side, dist)
            got(sib.at[0, j], sib_rs.at[0, j])
            parts = [sib.at[0, j]]
            for way in ((0, 1) if dist == 0 else (side,) if dist < 3 else ()):
                got(rrx.at[way, dist], rrx_rs.at[way, dist])
                parts.append(rrx.at[way, dist])

            @pl.when(lower)
            def _():
                got(yvx.at[j], yv_rs.at[j])
                add_into(dkv.at[0, j, k], parts + [yvx.at[j]])

            @pl.when(upper)
            def _():
                add_into(dkv.at[0, j, k], parts)

            if dist == 3:
                half = pl.ds(side * 96, 96)
                got(rrx.at[side, 3, half], rrx_rs.at[side, 3])
                add_into(dkv.at[0, j, k, half], [rrx.at[side, 3, half]])
        for side in ((0, 1) if dist > 0 else ()):
            def make(side=side):
                if dist == 4:
                    half = pl.ds(side * 96, 96)
                    src, dst = dkv.at[0, 4, k, half], rrx.at[side, 3, half]
                else:
                    src, dst = dkv.at[0, j_of(side, dist), k], rrx.at[side, dist - 1]
                return copy(src, dst, rrx_ss.at[side, dist - 1],
                            rrx_rs.at[side, dist - 1], ring[side])
            send(None, make)

    def proj_pass(dist):
        for side in sides_of(dist):
            j = j_of(side, dist)
            slot = pj_slot(j, k)
            got(pjs.at[j], pjs_rs.at[j])
            parts = [pjs.at[j]]
            if 0 < dist < 3:
                got(pjr.at[side, dist], pjr_rs.at[side, dist])
                parts.append(pjr.at[side, dist])
            elif dist == 0:
                for other in (0, 1):
                    got(pjr.at[other, 0], pjr_rs.at[other, 0])
                    parts.append(pjr.at[other, 0])
            add_into(pj.at[slot], parts)
            if dist == 3:
                half = pl.ds(side * 64, 64)
                got(pjr.at[side, 3, half], pjr_rs.at[side, 3])
                add_into(pj.at[slot, half], [pjr.at[side, 3, half]])
        if dist == 0:
            return
        for side in (0, 1):
            def make(side=side):
                if dist == 4:
                    half = pl.ds(side * 64, 64)
                    src, dst = pj.at[pj_slot(4, k), half], pjr.at[side, 3, half]
                else:
                    src, dst = pj.at[pj_slot(j_of(side, dist), k)], pjr.at[side, dist - 1]
                return copy(src, dst, pjr_ss.at[side, dist - 1],
                            pjr_rs.at[side, dist - 1], ring[side])
            send(None, make)

    got(attn.at[1], at_s.at[1])
    proj_terms(0, 2)
    proj_pass(4)
    proj_terms(2, NX)
    for j in range(NZ):
        pending.append((None, lambda j=j: proj_swap(j)))
    head_grads_done()
    backward_single(4)
    for dist in (3, 2, 1):
        @pl.when(upper)
        def _():
            backward_other_row(dist)
            kv_across(dist + 1)

        kv_pass(dist + 1)
        backward_own_row(dist)
        proj_pass(dist)

    backward_single(0)

    @pl.when(upper)
    def _():
        kv_across(1)

    kv_pass(1)

    query_rows = (dqt[...] * SCALE).T.astype(BF)
    empty = jnp.zeros((TOKENS - SLOTS, HEAD), BF)
    for h in range(HEADS):
        part = jnp.concatenate([query_rows[h * SLOTS:(h + 1) * SLOTS, :], empty], axis=0)
        qo_ref[:, h * HEAD:(h + 1) * HEAD] = mm(pickt[...], part).astype(BF)

    @pl.when(upper)
    def _():
        kv_across(0)

    proj_pass(0)
    po_ref[...] = pj[pj_slot(0, k)]
    kv_pass(0)
    sums = jnp.concatenate(
        [dkv[0, 0, k], jnp.zeros((TOKENS - SLOTS, 2 * HEAD), BF)], axis=0)
    kvo_ref[...] = mm(pickt[...], sums).astype(BF)

    for cond, make in pending:
        if cond is None:
            make().wait_send()
        else:
            @pl.when(cond)
            def _():
                make().wait_send()


def shards(queries, keys_values, upstream, out_proj, keep_index):
    keep = keep_index.reshape(1, SLOTS)
    dma = pltpu.SemaphoreType.DMA
    width = HEADS * HEAD
    vmem = pltpu.VMEM
    scratch = [
        vmem((4 * NZ, ROWS, 2 * HEAD), BF),
        vmem((2 * NZ, 128, width), BF),
        vmem((NX, 2, SLOTS, width), BF),
        vmem((SLOTS, width), BF),
        vmem((2 * NZ, PAIR, QROWS), BF),
        vmem((2 * NZ, 8, QROWS), F32),
        vmem((QROWS, HEAD), BF),
        vmem((QROWS, HEAD), BF),
        vmem((HEAD, QROWS), F32),
        vmem((HEAD, QROWS), F32),
        vmem((8, QROWS), F32),
        vmem((TOKENS, TOKENS), BF),
        vmem((2, SLOTS, width), BF),
        vmem((2, SLOTS, width), F32),
        vmem((SLOTS, width), BF),
        vmem((SLOTS, width), BF),
        vmem((8, TOKENS), jnp.int32),
        vmem((2 * NZ, 128, width), BF),
        vmem((NZ, 128, width), BF),
        vmem((2, 4, 128, width), BF),
        vmem((2, NZ, 2, SLOTS, 2 * HEAD), BF),
        vmem((2, NZ, SLOTS, 2 * HEAD), BF),
        vmem((2, 4, SLOTS, 2 * HEAD), BF),
        vmem((NZ, SLOTS, 2 * HEAD), BF),
        dma((2, 2, 5)), dma((2, 2, 5)), dma((2, 2, 5)), dma((2, 2, 5)),
        dma((2, 5)), dma((2, 5)), dma((2, 5)), dma((2, 5)),
        dma((2, 5)), dma((2, 5)), dma((2, 5)), dma((2, 5)),
        dma((2, 2, 3)), dma((2, 2, 3)), dma((2,)), dma((2,)), dma((2,)),
        dma((NZ,)), dma((NZ,)), dma((2, 4)), dma((2, 4)),
        dma((2, NZ)), dma((2, NZ)), dma((2, 4)), dma((2, 4)),
        dma((NZ,)), dma((NZ,)),
    ]
    return pl.pallas_call(
        kernel,
        out_shape=(
            jax.ShapeDtypeStruct(queries.shape, BF),
            jax.ShapeDtypeStruct(keys_values.shape, BF),
            jax.ShapeDtypeStruct(out_proj.shape, BF),
        ),
        in_specs=[pl.BlockSpec(memory_space=pltpu.VMEM)] * 5,
        out_specs=[pl.BlockSpec(memory_space=pltpu.VMEM)] * 3,
        scratch_shapes=scratch,
        compiler_params=pltpu.CompilerParams(
            collective_id=0, has_side_effects=True, vmem_limit_bytes=56 * 1024 * 1024
        ),
    )(keep, queries, keys_values, upstream, out_proj)


def solution(mesh):
    in_specs = (P("ctx", "tp"), P("ctx", "tp"), P("ctx", "tp"), P("ctx", "tp"), P("ctx"))
    out_specs = (P("ctx", "tp"), P("ctx", "tp"), P("ctx", "tp"))
    return jax.shard_map(shards, mesh=mesh, in_specs=in_specs, out_specs=out_specs, check_vma=False)
```
